256 devices in a mesh: inst: 32 (over z, y_lo, core), tp: 8 (over y_hi, x).
Axes of the slice: x: 4, y: 4 (y_hi: 2, y_lo: 2; y = y_hi * 2 + y_lo), z: 8, core: 2. Of those that a mesh axis runs over, the one named last changes fastest.
Arguments:
- prompt_q: bfloat16 [8192, 8192], P('inst', 'tp'), may hold values from -6 to 6
- prompt_k: bfloat16 [8192, 1024], P('inst', 'tp'), may hold values from -6 to 6
- prompt_value_rows: bfloat16 [8192, 1024], P('inst', 'tp'), may hold values from -6 to 6
- decode_q: bfloat16 [1024, 4, 8192], P('inst', None, 'tp'), may hold values from -6 to 6
- new_k: bfloat16 [1024, 4, 1024], P('inst', None, 'tp'), may hold values from -6 to 6
- new_v: bfloat16 [1024, 4, 1024], P('inst', None, 'tp'), may hold values from -6 to 6
- cache_k: bfloat16 [1024, 256, 1024], P('inst', None, 'tp'), may hold values from -6 to 6
- cache_v: bfloat16 [1024, 256, 1024], P('inst', None, 'tp'), may hold values from -6 to 6
- cache_len: int32 [1024], P('inst'), may hold values from 1 to 256, as said below
- pairing: int32 [32], replicated, may hold values from 0 to 31, each once
Outputs:
- prompt_out: bfloat16 [8192, 8192], P('inst', 'tp')
- decode_out: bfloat16 [1024, 4, 8192], P('inst', None, 'tp')
The draws below stay inside these ranges and needn't reach their ends.
Inputs may be any that keep to these rules, and one draw needn't show every extreme that they name: `cache_len`: every instance has a row whose cache is full, at 256 live slots. `pairing`: each instance's number is named once.
All inputs are finite; a program needn't handle non-finite values.
Results may differ from the reference program's by a relative error of at most 0.006.
Values may be sent and summed in bfloat16 or wider, within the bound.
A program may use at most 64 MiB of HBM per device.

```python
import jax
import jax.numpy as jnp
from jax import lax

HQ = 64
KV = 8
HDIM = 128
TOK_DEV = 256
ROWS_DEV = 32
CACHE = 256
STEPS = 4
TOKENS = 8192
ROWS = 1024
N_INST = 32


def base_normal(key, shape):
    return jnp.clip(jax.random.normal(key, shape, jnp.float32), -6.0, 6.0)


def draw_prompt_q(key, part):
    key = jax.random.fold_in(key, 11)
    shape = (TOKENS, HQ, HDIM)
    values = base_normal(key, shape)
    return values.reshape(TOKENS, HQ * HDIM).astype(jnp.bfloat16)


def draw_prompt_k(key, part):
    key = jax.random.fold_in(key, 12)
    shape = (TOKENS, KV, HDIM)
    values = base_normal(key, shape)
    return values.reshape(TOKENS, KV * HDIM).astype(jnp.bfloat16)


def draw_decode_q(key, part):
    key = jax.random.fold_in(key, 13)
    shape = (ROWS, STEPS, HQ, HDIM)
    values = base_normal(key, shape)
    return values.reshape(ROWS, STEPS, HQ * HDIM).astype(jnp.bfloat16)


def draw_cache_k(key, part):
    key = jax.random.fold_in(key, 14)
    shape = (ROWS, CACHE, KV, HDIM)
    values = base_normal(key, shape)
    return values.reshape(ROWS, CACHE, KV * HDIM).astype(jnp.bfloat16)


def draw_new_k(key, part):
    key = jax.random.fold_in(key, 15)
    shape = (ROWS, STEPS, KV, HDIM)
    values = base_normal(key, shape)
    return values.reshape(ROWS, STEPS, KV * HDIM).astype(jnp.bfloat16)


def draw_cache_len(key, part):
    key = jax.random.fold_in(key, 3)
    first, second = jax.random.split(key)
    lengths = jax.random.randint(first, (ROWS_DEV * N_INST,), 1, CACHE + 1)
    offsets = jax.random.randint(second, (N_INST,), 0, ROWS_DEV)
    full_block_slots = jnp.arange(ROWS_DEV * N_INST) % ROWS_DEV == jnp.repeat(offsets, ROWS_DEV)
    return jnp.where(full_block_slots, CACHE, lengths).astype(jnp.int32)


def steps_of(own_key, extent, cuts, smallest, largest):
    level, own = 1.0, jax.random.fold_in(own_key, 6)
    for position, parts in cuts:
        heights = jnp.exp(jax.random.uniform(jax.random.fold_in(own, position), (parts,), jnp.float32, smallest / len(cuts), largest / len(cuts)))
        level = level * jnp.repeat(heights, extent[position] // parts).reshape([-1 if axis == position else 1 for axis in range(len(extent))])
    return level


def normal_values(rng, shape, scale, limit, shards=(), kind=jnp.bfloat16):
    level = steps_of(rng, shape, shards, -0.22, 0.18) if shards else 1.0
    entries = jax.random.normal(rng, shape, jnp.float32) * scale * level
    return jnp.minimum(jnp.maximum(entries, -limit), limit).astype(kind)


def setup_inputs(seed: int = 0) -> dict:
    streams_of = jax.random.split(jax.random.key(seed), 11)
    prompt_q = draw_prompt_q(jax.random.fold_in(streams_of[10], 71), 0)
    prompt_k = draw_prompt_k(jax.random.fold_in(streams_of[10], 71), 0)
    prompt_value_rows = normal_values(streams_of[2], (TOKENS, KV * HDIM), 1.0, 6.0, ((0, 32), (1, 8)))
    decode_q = draw_decode_q(jax.random.fold_in(streams_of[10], 71), 0)
    new_k = draw_new_k(jax.random.fold_in(streams_of[10], 71), 0)
    new_v = normal_values(streams_of[5], (ROWS, STEPS, KV * HDIM), 1.0, 6.0, ((0, 32), (2, 8)))
    cache_k = draw_cache_k(jax.random.fold_in(streams_of[10], 71), 0)
    cache_v = normal_values(streams_of[7], (ROWS, CACHE, KV * HDIM), 1.0, 6.0, ((0, 32), (2, 8)))
    cache_len = draw_cache_len(jax.random.fold_in(streams_of[10], 71), 0)
    pairing = jax.random.permutation(streams_of[9], N_INST).astype(jnp.int32)
    return dict(prompt_q=prompt_q, prompt_k=prompt_k, prompt_value_rows=prompt_value_rows, decode_q=decode_q, new_k=new_k, new_v=new_v, cache_k=cache_k, cache_v=cache_v, cache_len=cache_len, pairing=pairing)


NEG = -1e30


def prompt_attention(prompt_q, prompt_k, prompt_value_rows):
    ratio = HQ // KV
    scale = HDIM ** -0.5
    blocks = TOKENS // TOK_DEV
    qh = prompt_q.reshape(blocks, TOK_DEV, KV, ratio, HDIM).transpose(2, 0, 1, 3, 4)
    kh = prompt_k.reshape(TOKENS, KV, HDIM).transpose(1, 0, 2)
    vh = prompt_value_rows.reshape(TOKENS, KV, HDIM).transpose(1, 0, 2)
    key_pos = jnp.arange(TOKENS, dtype=jnp.int32)

    def one_head(args):
        qg, kg, vg = args

        def one_block(inner):
            qb, index = inner
            scores = jnp.einsum('trd,sd->rts', qb.astype(jnp.float32), kg.astype(jnp.float32)) * scale
            query_pos = index * TOK_DEV + jnp.arange(TOK_DEV, dtype=jnp.int32)
            keep = key_pos[None, :] <= query_pos[:, None]
            scores = jnp.where(keep[None], scores, NEG)
            top = jnp.max(scores, axis=-1, keepdims=True)
            attention_weights = jnp.where(keep[None], jnp.exp(scores - top), 0.0)
            total = jnp.sum(attention_weights, axis=-1)
            rounded = attention_weights.astype(jnp.bfloat16).astype(jnp.float32)
            summed = jnp.einsum('rts,sd->rtd', rounded, vg.astype(jnp.float32))
            return (summed / total[..., None]).transpose(1, 0, 2)

        return lax.map(one_block, (qg, jnp.arange(blocks, dtype=jnp.int32)))

    out = lax.map(one_head, (qh, kh, vh))
    return out.transpose(1, 2, 0, 3, 4).reshape(TOKENS, HQ * HDIM).astype(jnp.bfloat16)


def decode_group(dec_q, nk, nv, ck, cv, clen, pk, pv):
    rows, steps = dec_q.shape[0], dec_q.shape[1]
    groups = nk.shape[-1] // HDIM
    ratio = dec_q.shape[-1] // (groups * HDIM)
    slots = ck.shape[1]
    plen = pk.shape[0]
    scale = HDIM ** -0.5
    query = dec_q.reshape(rows, steps, groups, ratio, HDIM).astype(jnp.float32)
    ckf = ck.reshape(rows, slots, groups, HDIM).astype(jnp.float32)
    cvf = cv.reshape(rows, slots, groups, HDIM).astype(jnp.float32)
    pkf = pk.reshape(plen, groups, HDIM).astype(jnp.float32)
    pvf = pv.reshape(plen, groups, HDIM).astype(jnp.float32)
    nkf = nk.reshape(rows, steps, groups, HDIM).astype(jnp.float32)
    nvf = nv.reshape(rows, steps, groups, HDIM).astype(jnp.float32)
    cache_keep = jnp.arange(slots, dtype=jnp.int32)[None, :] < clen[:, None]
    cache_keep = cache_keep[:, None, None, None, :]
    step_keep = jnp.arange(steps, dtype=jnp.int32)[None, :] <= jnp.arange(steps, dtype=jnp.int32)[:, None]
    step_keep = step_keep[None, :, None, None, :]
    s_cache = jnp.where(cache_keep, jnp.einsum('asgrd,acgd->asgrc', query, ckf) * scale, NEG)
    s_prompt = jnp.einsum('asgrd,pgd->asgrp', query, pkf) * scale
    s_new = jnp.where(step_keep, jnp.einsum('asgrd,atgd->asgrt', query, nkf) * scale, NEG)
    top = jnp.maximum(jnp.maximum(jnp.max(s_cache, -1), jnp.max(s_prompt, -1)), jnp.max(s_new, -1))[..., None]
    p_cache = jnp.where(cache_keep, jnp.exp(s_cache - top), 0.0)
    p_prompt = jnp.exp(s_prompt - top)
    p_new = jnp.where(step_keep, jnp.exp(s_new - top), 0.0)
    total = jnp.sum(p_cache, -1) + jnp.sum(p_prompt, -1) + jnp.sum(p_new, -1)
    summed = jnp.einsum('asgrc,acgd->asgrd', p_cache.astype(jnp.bfloat16).astype(jnp.float32), cvf)
    summed = summed + jnp.einsum('asgrp,pgd->asgrd', p_prompt.astype(jnp.bfloat16).astype(jnp.float32), pvf)
    summed = summed + jnp.einsum('asgrt,atgd->asgrd', p_new.astype(jnp.bfloat16).astype(jnp.float32), nvf)
    out = summed / total[..., None]
    return out.reshape(rows, steps, groups * ratio * HDIM).astype(jnp.bfloat16)


def reference(prompt_q, prompt_k, prompt_value_rows, decode_q, new_k, new_v, cache_k, cache_v, cache_len, pairing):
    prompt_out = prompt_attention(prompt_q, prompt_k, prompt_value_rows)

    def single_instance_body(index):
        first = index * ROWS_DEV
        source = (pairing[index] * TOK_DEV).astype(jnp.int32)
        pick = lambda arr: lax.dynamic_slice_in_dim(arr, first, ROWS_DEV, 0)
        pk = lax.dynamic_slice_in_dim(prompt_k, source, TOK_DEV, 0)
        pv = lax.dynamic_slice_in_dim(prompt_value_rows, source, TOK_DEV, 0)
        return decode_group(pick(decode_q), pick(new_k), pick(new_v), pick(cache_k), pick(cache_v), pick(cache_len), pk, pv)

    decode_out = lax.map(single_instance_body, jnp.arange(N_INST, dtype=jnp.int32))
    decode_out = decode_out.reshape(ROWS, STEPS, HQ * HDIM)
    return prompt_out, decode_out
```

```python
import math

import jax
import jax.numpy as jnp
from jax import lax
from jax.experimental import pallas as pl
from jax.experimental.pallas import tpu as pltpu
from jax.sharding import PartitionSpec as P

MESH = pl.DeviceIdType.MESH
BF16 = jnp.bfloat16
F32 = jnp.float32

HDIM = 128
HEADS = 8
TOK = 256
ROWS = 32
CACHE = 256
STEPS = 4
NZ = 8
NINST = 32
CELL = 4 * TOK
NEG = -1e30
FACTOR = HDIM**-0.5 * math.log2(math.e)

ROUTE = {}
for _d in (1, 2, 3):
    for _part in (0, 1):
        ROUTE["A", -_d, _part] = "down"
        ROUTE["A", _d, _part] = "up"
    ROUTE["B", -_d, 0] = "down"
    ROUTE["B", _d, 1] = "up"
    ROUTE["B", _d, 0] = "side"
    ROUTE["B", -_d, 1] = "side"
ROUTE["A", -4, 0] = "down"
ROUTE["A", 4, 1] = "up"
ROUTE["B", 0, 0] = "side"
ROUTE["B", 0, 1] = "side"
ROUTE["B", -4, 0] = "side"
ROUTE["B", 4, 1] = "side"

EVENTS_NEAR = [("A", -1, 0), ("A", 1, 0), ("A", -1, 1), ("A", 1, 1)]
EVENTS_SIDE = [("B", 0, 0), ("B", 0, 1)]
EVENTS_OWN = [
    ("B", 1, 0),
    ("A", -2, 0),
    ("A", 2, 0),
    ("A", -2, 1),
    ("A", 2, 1),
    ("B", -1, 1),
]
EVENTS_LOOP = [
    [("B", -1, 0), ("B", 1, 1)],
    [("B", 2, 0), ("B", -2, 1)],
    [("A", -3, 0), ("A", 3, 1), ("A", -3, 1), ("A", 3, 0)],
    [("B", -2, 0), ("B", 2, 1)],
    [("B", 3, 0), ("B", -3, 1), ("A", -4, 0), ("A", 4, 1)],
    [("B", -3, 0), ("B", 3, 1)],
    [("B", -4, 0), ("B", 4, 1)],
]
CELL_ORDER = (-1, 1, -2, 2, -3, 3, 4)


def forwards(item):
    col, d, part = item
    to = []
    if ROUTE.get((col, d - 1, part)) == "down":
        to.append("up")
    if ROUTE.get((col, d + 1, part)) == "up":
        to.append("down")
    if col == "A" and ROUTE.get(("B", d, part)) == "side":
        to.append("side")
    to.append("twin")
    return to


OWN = [("A", 0, 0), ("A", 0, 1)]
SENDS = [(item, to) for item in OWN + list(ROUTE) for to in forwards(item)]
SEND_INDEX = {key: i for i, key in enumerate(SENDS)}


def kernel(
    q_hbm, k_hbm, v_hbm, dq_hbm, nk_hbm, nv_hbm, ck_hbm, cv_hbm, clen_ref, pair_ref,
    o_hbm, do_hbm,
    kv, q, dq, nk, nv, ck, cv, qs, acc, top, vd, dqf, dqs, dacc, dtop, nkf, nvf, out, dout,
    send_sem, recv_sem, local_sem, cache_sem,
):
    me = lax.axis_index("inst")
    core = lax.rem(me, 2)
    y = lax.rem(me // 2, 2)
    z = me // 4

    def slot(col, d):
        zz = lax.rem(z + (d + NZ), NZ)
        yy = y if col == "A" else 1 - y
        return 4 * zz + 2 * yy + core

    device = {
        "up": 4 * lax.rem(z + 1, NZ) + 2 * y + core,
        "down": 4 * lax.rem(z + NZ - 1, NZ) + 2 * y + core,
        "side": 4 * z + 2 * (1 - y) + core,
        "twin": 4 * z + 2 * y + 1 - core,
    }

    def remote(item, to):
        col, d, part = item
        place = slot(col, d)
        return pltpu.make_async_remote_copy(
            src_ref=kv.at[place, part],
            dst_ref=kv.at[place, part],
            send_sem=send_sem.at[SEND_INDEX[item, to]],
            recv_sem=recv_sem.at[place, part],
            device_id={"inst": device[to]},
            device_id_type=MESH,
        )

    def arrived(place, part):
        pltpu.make_async_remote_copy(
            src_ref=kv.at[place, part],
            dst_ref=kv.at[place, part],
            send_sem=send_sem.at[0],
            recv_sem=recv_sem.at[place, part],
            device_id={"inst": device["twin"]},
            device_id_type=MESH,
        ).wait_recv()

    def events(items):
        for item in items:
            arrived(slot(item[0], item[1]), item[2])
            for to in forwards(item):
                remote(item, to).start()

    def twin_cell(zz):
        for yy in (0, 1):
            place = 4 * zz + 2 * yy + 1 - core
            arrived(place, 0)
            arrived(place, 1)

    own = [
        pltpu.make_async_copy(k_hbm, kv.at[me, 0], local_sem.at[0]),
        pltpu.make_async_copy(v_hbm, kv.at[me, 1], local_sem.at[1]),
    ]
    small = [
        pltpu.make_async_copy(dq_hbm, dq, local_sem.at[2]),
        pltpu.make_async_copy(nk_hbm, nk, local_sem.at[3]),
        pltpu.make_async_copy(nv_hbm, nv, local_sem.at[4]),
    ]
    queries = pltpu.make_async_copy(q_hbm, q, local_sem.at[5])

    def cache_copies(g):
        rows = pl.ds(8 * g, 8)
        return (
            pltpu.make_async_copy(ck_hbm.at[rows], ck.at[rows], cache_sem.at[g, 0]),
            pltpu.make_async_copy(cv_hbm.at[rows], cv.at[rows], cache_sem.at[g, 1]),
        )

    for copy in own + small:
        copy.start()
    for g in range(4):
        for copy in cache_copies(g):
            copy.start()
    queries.start()

    barrier = pltpu.get_barrier_semaphore()
    for to in ("up", "down", "side", "twin"):
        pl.semaphore_signal(barrier, inc=1, device_id={"inst": device[to]}, device_id_type=MESH)
    pl.semaphore_wait(barrier, 4)

    for part in (0, 1):
        own[part].wait()
        for to in forwards(OWN[part]):
            remote(OWN[part], to).start()

    for copy in small:
        copy.wait()
    for h in range(HEADS):
        dqf[:, pl.ds(h, STEPS, stride=HEADS), :] = dq[:, :, h * HDIM : (h + 1) * HDIM].astype(F32)
    dqs[...] = dqf[...].astype(BF16)
    for a in range(ROWS):
        nkf[a * STEPS : (a + 1) * STEPS, :] = nk[a].astype(F32)
        nvf[a * STEPS : (a + 1) * STEPS, :] = nv[a].astype(F32)
    vd[:, HDIM:] = jnp.ones((CELL, HDIM), BF16)

    def dot_t(a, b):
        return lax.dot_general(a, b, (((1,), (1,)), ((), ())), preferred_element_type=F32)

    def wide(x, width):
        return jnp.concatenate([x] * (width // HDIM), axis=1)

    ones = jnp.ones((CACHE, HDIM), BF16)

    def decode_rows(g):
        for copy in cache_copies(g):
            copy.wait()
        for u in range(8):
            a = 8 * g + u
            scores = dot_t(dqs[a], ck[a]) * FACTOR
            live = lax.broadcasted_iota(jnp.int32, scores.shape, 1) < clen_ref[a]
            scores = jnp.where(live, scores, NEG)
            peak = jnp.max(scores, axis=1, keepdims=True)
            p = jnp.exp2(scores - peak).astype(BF16)
            dtop[a] = jnp.broadcast_to(peak, (STEPS * HEADS, HDIM))
            dacc[a] = jnp.dot(
                p, jnp.concatenate([cv[a], ones], axis=1), preferred_element_type=F32
            )

    def decode_pair(g, _):
        decode_rows(g)
        return 0

    lax.fori_loop(0, 2, decode_pair, 0)
    events(EVENTS_NEAR)
    lax.fori_loop(2, 4, decode_pair, 0)
    events(EVENTS_SIDE)

    queries.wait()
    for h in range(HEADS):
        qs[h] = q[:, h * HDIM : (h + 1) * HDIM]
    twin_cell(z)

    def cell_keys(zz):
        return kv[pl.ds(4 * zz, 4), 0].reshape(CELL, HDIM)

    def load_values(zz):
        vd[:, :HDIM] = kv[pl.ds(4 * zz, 4), 1].reshape(CELL, HDIM)

    load_values(z)

    def first_cell(half):
        for u in range(HEADS // 2):
            h = half * (HEADS // 2) + u
            scores = dot_t(qs[h], cell_keys(z)) * FACTOR
            key = lax.broadcasted_iota(jnp.int32, scores.shape, 1)
            row = lax.broadcasted_iota(jnp.int32, scores.shape, 0)
            scores = jnp.where(key <= row + TOK * lax.rem(me, 4), scores, NEG)
            peak = jnp.max(scores, axis=1, keepdims=True)
            p = jnp.exp2(scores - peak).astype(BF16)
            top[h] = jnp.broadcast_to(peak, (TOK, HDIM))
            acc[h] = jnp.dot(p, vd[...], preferred_element_type=F32)

    def first_half(half, _):
        first_cell(half)

        @pl.when(half == 0)
        def _():
            events(EVENTS_OWN)

        return 0

    lax.fori_loop(0, 2, first_half, 0)

    def merge(scores, values, top_ref, acc_ref, index):
        before = top_ref[index]
        peak = jnp.maximum(before, jnp.max(scores, axis=1, keepdims=True))
        top_ref[index] = peak
        p = jnp.exp2(scores - wide(peak, scores.shape[1])).astype(BF16)
        scale = jnp.exp2(before - peak)
        return wide(scale, 2 * HDIM) * acc_ref[index] + jnp.dot(
            p, values, preferred_element_type=F32
        )

    def cell_step(t, _):
        half = lax.rem(t, 2)
        j = t // 2
        for i, items in enumerate(EVENTS_LOOP):

            @pl.when(t == i)
            def _(items=items):
                events(items)

        away = j // 2 + 1
        zz = lax.rem(z + NZ + jnp.where(lax.rem(j, 2) == 0, -away, away), NZ)

        @pl.when(half == 0)
        def _():
            twin_cell(zz)

        @pl.when(zz < z)
        def _():
            @pl.when(half == 0)
            def _():
                load_values(zz)

            for u in range(HEADS // 2):
                h = half * (HEADS // 2) + u
                scores = dot_t(qs[h], cell_keys(zz)) * FACTOR
                acc[h] = merge(scores, vd[...], top, acc, h)

        return 0

    lax.fori_loop(0, 14, cell_step, 0)

    for h in range(HEADS):
        out[:, h * HDIM : (h + 1) * HDIM] = (acc[h, :, :HDIM] / acc[h, :, HDIM:]).astype(BF16)
    out_copy = pltpu.make_async_copy(out, o_hbm, local_sem.at[6])
    out_copy.start()

    pair = pair_ref[me]
    new_keys = ROWS * STEPS
    keys = jnp.concatenate([kv[pair, 0], nkf[...].astype(BF16)], axis=0)
    vd[:TOK, :HDIM] = kv[pair, 1]
    vd[TOK : TOK + new_keys, :HDIM] = nvf[...].astype(BF16)
    values = vd[: TOK + new_keys, :]
    per = STEPS * HEADS

    def decode_last(g, _):
        rows = pl.ds(8 * g, 8)
        size = 8 * per
        scores = dot_t(dqs[rows].reshape(size, HDIM), keys) * FACTOR
        column = lax.broadcasted_iota(jnp.int32, (size, new_keys), 1)
        row = lax.broadcasted_iota(jnp.int32, (size, new_keys), 0) + g * size
        keep = jnp.logical_and(
            column // STEPS == row // per,
            lax.rem(column, STEPS) <= lax.rem(row // HEADS, STEPS),
        )
        fresh = jnp.where(keep, scores[:, TOK:], NEG)
        scores = jnp.concatenate([scores[:, :TOK], fresh], axis=1)
        before = dtop[rows].reshape(size, HDIM)
        peak = jnp.maximum(before, jnp.max(scores, axis=1, keepdims=True))
        p = jnp.exp2(scores - wide(peak, TOK + new_keys)).astype(BF16)
        total = wide(jnp.exp2(before - peak), 2 * HDIM) * dacc[rows].reshape(size, 2 * HDIM)
        total = total + jnp.dot(p, values, preferred_element_type=F32)
        dqf[rows] = (total[:, :HDIM] / total[:, HDIM:]).reshape(8, per, HDIM)
        return 0

    lax.fori_loop(0, 4, decode_last, 0)
    for h in range(HEADS):
        dout[:, :, h * HDIM : (h + 1) * HDIM] = dqf[:, pl.ds(h, STEPS, stride=HEADS), :].astype(BF16)
    dout_copy = pltpu.make_async_copy(dout, do_hbm, local_sem.at[7])
    dout_copy.start()
    for item, to in SENDS:
        remote(item, to).wait_send()
    out_copy.wait()
    dout_copy.wait()


def per_device(*args):
    any_spec = pl.BlockSpec(memory_space=pl.ANY)
    smem = pl.BlockSpec(memory_space=pltpu.SMEM)
    vmem = pltpu.VMEM
    per = STEPS * HEADS
    return pl.pallas_call(
        kernel,
        out_shape=(
            jax.ShapeDtypeStruct((TOK, HEADS * HDIM), BF16),
            jax.ShapeDtypeStruct((ROWS, STEPS, HEADS * HDIM), BF16),
        ),
        in_specs=[any_spec] * 8 + [smem, smem],
        out_specs=(any_spec, any_spec),
        scratch_shapes=[
            vmem((NINST, 2, TOK, HDIM), BF16),
            vmem((TOK, HEADS * HDIM), BF16),
            vmem((ROWS, STEPS, HEADS * HDIM), BF16),
            vmem((ROWS, STEPS, HDIM), BF16),
            vmem((ROWS, STEPS, HDIM), BF16),
            vmem((ROWS, CACHE, HDIM), BF16),
            vmem((ROWS, CACHE, HDIM), BF16),
            vmem((HEADS, TOK, HDIM), BF16),
            vmem((HEADS, TOK, 2 * HDIM), F32),
            vmem((HEADS, TOK, HDIM), F32),
            vmem((CELL, 2 * HDIM), BF16),
            vmem((ROWS, per, HDIM), F32),
            vmem((ROWS, per, HDIM), BF16),
            vmem((ROWS, per, 2 * HDIM), F32),
            vmem((ROWS, per, HDIM), F32),
            vmem((ROWS * STEPS, HDIM), F32),
            vmem((ROWS * STEPS, HDIM), F32),
            vmem((TOK, HEADS * HDIM), BF16),
            vmem((ROWS, STEPS, HEADS * HDIM), BF16),
            pltpu.SemaphoreType.DMA((len(SENDS),)),
            pltpu.SemaphoreType.DMA((NINST, 2)),
            pltpu.SemaphoreType.DMA((8,)),
            pltpu.SemaphoreType.DMA((4, 2)),
        ],
        compiler_params=pltpu.CompilerParams(
            collective_id=0, has_side_effects=True, vmem_limit_bytes=56 * 2**20
        ),
    )(*args)


def solution(mesh):
    return jax.shard_map(
        per_device,
        mesh=mesh,
        in_specs=(
            P("inst", "tp"),
            P("inst", "tp"),
            P("inst", "tp"),
            P("inst", None, "tp"),
            P("inst", None, "tp"),
            P("inst", None, "tp"),
            P("inst", None, "tp"),
            P("inst", None, "tp"),
            P("inst"),
            P(),
        ),
        out_specs=(P("inst", "tp"), P("inst", None, "tp")),
        check_vma=False,
    )
```

```python
import math

import jax
import jax.numpy as jnp
from jax import lax
from jax.experimental import pallas as pl
from jax.experimental.pallas import tpu as pltpu
from jax.sharding import PartitionSpec as P

MESH = pl.DeviceIdType.MESH
BF16 = jnp.bfloat16
F32 = jnp.float32

HDIM = 128
HEADS = 8
TOK = 256
ROWS = 32
CACHE = 256
STEPS = 4
NZ = 8
NINST = 32
CHIP = 2 * TOK
NEG = -1e30
FACTOR = HDIM**-0.5 * math.log2(math.e)

ROUTE = {}
for _d in (1, 2, 3):
    for _part in (0, 1):
        ROUTE["A", -_d, _part] = "down"
        ROUTE["A", _d, _part] = "up"
    ROUTE["B", -_d, 0] = "down"
    ROUTE["B", _d, 1] = "up"
    ROUTE["B", _d, 0] = "side"
    ROUTE["B", -_d, 1] = "side"
ROUTE["A", -4, 0] = "down"
ROUTE["A", 4, 1] = "up"
ROUTE["B", 0, 0] = "side"
ROUTE["B", 0, 1] = "side"
ROUTE["B", -4, 0] = "side"
ROUTE["B", 4, 1] = "side"

HEAD = [
    ([], 'dec'),
    ([('A', 1, 0), ('A', -1, 0), ('A', -1, 1), ('A', 1, 1)], 'own'),
    ([('B', 0, 1), ('B', 0, 0)], 'dec'),
]
PLAN = [
    ([('A', 2, 0), ('A', 2, 1), ('A', -2, 1), ('A', -2, 0)], [('A', -1)]),
    ([('B', 1, 1), ('B', -1, 1), ('B', -1, 0)], [('A', 2), ('A', 1)]),
    ([('A', -3, 1), ('B', 2, 0), ('B', 1, 0), ('A', 3, 0), ('A', 3, 1), ('A', -3, 0)], [('B', 0), ('B', -1)]),
    ([('B', -2, 1), ('B', -2, 0)], [('B', 1), ('A', -3)]),
    ([('B', 2, 1), ('A', -4, 0), ('A', 4, 1), ('B', -3, 1), ('B', -3, 0)], [('B', -2), ('A', -2)]),
    ([], [('B', -3), ('B', 2)]),
    ([('B', -4, 0), ('B', 4, 1), ('B', 3, 1), ('B', 3, 0)], [('A', 3), ('A', 4)]),
    ([], [('B', 3), ('B', 4)]),
]
TAIL = []


def forwards(item):
    col, d, part = item
    to = []
    if ROUTE.get((col, d - 1, part)) == "down":
        to.append("up")
    if ROUTE.get((col, d + 1, part)) == "up":
        to.append("down")
    if col == "A" and ROUTE.get(("B", d, part)) == "side":
        to.append("side")
    return to


OWN = [("A", 0, 0), ("A", 0, 1)]
SENDS = [(item, to) for item in OWN + list(ROUTE) for to in forwards(item)]
CHIPS = [(col, d) for col in ("A", "B") for d in (-3, -2, -1, 0, 1, 2, 3, 4)]
SEND_INDEX = {key: i for i, key in enumerate(SENDS)}


def kernel(
    q_hbm, k_hbm, v_hbm, dq_hbm, nk_hbm, nv_hbm, ck_hbm, cv_hbm, clen_ref, pair_ref,
    out, dout,
    kv, q, dq, nk, nv, ck, cv, qs, acc, top, vd, dqf, dqs, dacc, dtop, nkf, nvf,
    send_sem, recv_sem, twin_send, twin_recv, local_sem, cache_sem,
):
    me = lax.axis_index("inst")
    core = lax.rem(me, 2)
    y = lax.rem(me // 2, 2)
    z = me // 4

    def slot(col, d):
        zz = lax.rem(z + (d + NZ), NZ)
        yy = y if col == "A" else 1 - y
        return 4 * zz + 2 * yy + core

    device = {
        "up": 4 * lax.rem(z + 1, NZ) + 2 * y + core,
        "down": 4 * lax.rem(z + NZ - 1, NZ) + 2 * y + core,
        "side": 4 * z + 2 * (1 - y) + core,
        "twin": 4 * z + 2 * y + 1 - core,
    }

    def remote(item, to):
        col, d, part = item
        place = slot(col, d)
        return pltpu.make_async_remote_copy(
            src_ref=kv.at[place, part],
            dst_ref=kv.at[place, part],
            send_sem=send_sem.at[SEND_INDEX[item, to]],
            recv_sem=recv_sem.at[place, part],
            device_id={"inst": device[to]},
            device_id_type=MESH,
        )

    def twin(col, d):
        place = slot(col, d)
        return pltpu.make_async_remote_copy(
            src_ref=kv.at[place],
            dst_ref=kv.at[place],
            send_sem=twin_send.at[CHIPS.index((col, d))],
            recv_sem=twin_recv.at[place],
            device_id={"inst": device["twin"]},
            device_id_type=MESH,
        )

    half = set()

    def arrived(place, part):
        pltpu.make_async_remote_copy(
            src_ref=kv.at[place, part],
            dst_ref=kv.at[place, part],
            send_sem=send_sem.at[0],
            recv_sem=recv_sem.at[place, part],
            device_id={"inst": device["twin"]},
            device_id_type=MESH,
        ).wait_recv()

    def events(items):
        for item in items:
            arrived(slot(item[0], item[1]), item[2])
            for to in forwards(item):
                remote(item, to).start()
            chip = (item[0], abs(item[1]) if abs(item[1]) == 4 else item[1])
            if chip in half:
                twin(*chip).start()
            half.add(chip)

    def twin_chip(col, d):
        place = slot(col, d) + 1 - 2 * core
        pltpu.make_async_remote_copy(
            src_ref=kv.at[place],
            dst_ref=kv.at[place],
            send_sem=twin_send.at[0],
            recv_sem=twin_recv.at[place],
            device_id={"inst": device["twin"]},
            device_id_type=MESH,
        ).wait_recv()

    own = [
        pltpu.make_async_copy(k_hbm, kv.at[me, 0], local_sem.at[0]),
        pltpu.make_async_copy(v_hbm, kv.at[me, 1], local_sem.at[1]),
    ]
    small = [
        pltpu.make_async_copy(dq_hbm, dq, local_sem.at[2]),
        pltpu.make_async_copy(nk_hbm, nk, local_sem.at[3]),
        pltpu.make_async_copy(nv_hbm, nv, local_sem.at[4]),
    ]
    queries = pltpu.make_async_copy(q_hbm, q, local_sem.at[5])

    def cache_copies(g):
        rows = pl.ds(8 * g, 8)
        return (
            pltpu.make_async_copy(ck_hbm.at[rows], ck.at[rows], cache_sem.at[g, 0]),
            pltpu.make_async_copy(cv_hbm.at[rows], cv.at[rows], cache_sem.at[g, 1]),
        )

    for copy in own + small:
        copy.start()
    for g in range(4):
        for copy in cache_copies(g):
            copy.start()
    queries.start()

    barrier = pltpu.get_barrier_semaphore()
    for to in ("up", "down", "side", "twin"):
        pl.semaphore_signal(barrier, inc=1, device_id={"inst": device[to]}, device_id_type=MESH)
    pl.semaphore_wait(barrier, 4)

    for part in (0, 1):
        own[part].wait()
        for to in forwards(OWN[part]):
            remote(OWN[part], to).start()
    twin("A", 0).start()

    for copy in small:
        copy.wait()
    for h in range(HEADS):
        dqf[:, pl.ds(h, STEPS, stride=HEADS), :] = dq[:, :, h * HDIM : (h + 1) * HDIM].astype(F32)
    dqs[...] = dqf[...].astype(BF16)
    for a in range(ROWS):
        nkf[a * STEPS : (a + 1) * STEPS, :] = nk[a].astype(F32)
        nvf[a * STEPS : (a + 1) * STEPS, :] = nv[a].astype(F32)
    vd[:, HDIM:] = jnp.ones((2 * CHIP, HDIM), BF16)

    def dot_t(a, b):
        return lax.dot_general(a, b, (((1,), (1,)), ((), ())), preferred_element_type=F32)

    def wide(x, width):
        return jnp.concatenate([x] * (width // HDIM), axis=1)

    ones = jnp.ones((CACHE, HDIM), BF16)

    def decode_rows(g):
        for copy in cache_copies(g):
            copy.wait()
        for u in range(8):
            a = 8 * g + u
            scores = dot_t(dqs[a], ck[a]) * FACTOR
            live = lax.broadcasted_iota(jnp.int32, scores.shape, 1) < clen_ref[a]
            scores = jnp.where(live, scores, NEG)
            peak = jnp.max(scores, axis=1, keepdims=True)
            p = jnp.exp2(scores - peak).astype(BF16)
            dtop[a] = jnp.broadcast_to(peak, (STEPS * HEADS, HDIM))
            dacc[a] = jnp.dot(
                p, jnp.concatenate([cv[a], ones], axis=1), preferred_element_type=F32
            )

    def decode_pair(g, _):
        decode_rows(g)
        return 0

    def chip_keys(chip):
        return kv[pl.ds(2 * chip, 2), 0].reshape(CHIP, HDIM)

    def load_values(chip, at):
        vd[at * CHIP : (at + 1) * CHIP, :HDIM] = kv[pl.ds(2 * chip, 2), 1].reshape(CHIP, HDIM)

    def own_chip():
        queries.wait()
        for h in range(HEADS):
            qs[h] = q[:, h * HDIM : (h + 1) * HDIM]
        twin_chip("A", 0)
        chip = me // 2
        load_values(chip, 0)
        for h in range(HEADS):
            scores = dot_t(qs[h], chip_keys(chip))
            key = lax.broadcasted_iota(jnp.int32, scores.shape, 1)
            row = lax.broadcasted_iota(jnp.int32, scores.shape, 0)
            scores = jnp.where(key <= row + TOK * core, scores, NEG)
            peak = jnp.max(scores, axis=1, keepdims=True) * FACTOR
            p = jnp.exp2(scores * FACTOR - peak).astype(BF16)
            top[h] = jnp.broadcast_to(peak, (TOK, HDIM))
            acc[h] = jnp.dot(p, vd[:CHIP], preferred_element_type=F32)

    done = 0
    for items, what in HEAD:
        events(items)
        if what == "dec":
            lax.fori_loop(done, done + 2, decode_pair, 0)
            done += 2
        else:
            own_chip()

    def merge(scores, values, top_ref, acc_ref, index):
        before = top_ref[index]
        peak = jnp.maximum(before, jnp.max(scores, axis=1, keepdims=True) * FACTOR)
        top_ref[index] = peak
        p = jnp.exp2(scores * FACTOR - wide(peak, scores.shape[1])).astype(BF16)
        scale = jnp.exp2(before - peak)
        return wide(scale, 2 * HDIM) * acc_ref[index] + jnp.dot(
            p, values, preferred_element_type=F32
        )

    def chip_of(col, d):
        return 2 * lax.rem(z + d + NZ, NZ) + (y if col == "A" else 1 - y)

    def step(t, _):
        for i, (items, chips) in enumerate(PLAN):

            @pl.when(t == i)
            def _(items=items, chips=chips):
                events(items)
                for chip in chips:
                    twin_chip(*chip)

        left = chip_of(*PLAN[0][1][0])
        right = chip_of(*PLAN[0][1][-1])
        paired = len(PLAN[0][1]) - 1
        for i, (_, chips) in enumerate(PLAN[1:], 1):
            left = jnp.where(t == i, chip_of(*chips[0]), left)
            right = jnp.where(t == i, chip_of(*chips[-1]), right)
            paired = jnp.where(t == i, len(chips) - 1, paired)
        mine = me // 2
        left_seen = left < mine
        right_seen = jnp.logical_and(right < mine, paired == 1)

        @pl.when(jnp.logical_and(left_seen, right_seen))
        def _():
            load_values(left, 0)
            load_values(right, 1)
            for h in range(HEADS):
                keys = jnp.concatenate([chip_keys(left), chip_keys(right)], axis=0)
                acc[h] = merge(dot_t(qs[h], keys), vd[...], top, acc, h)

        @pl.when(jnp.logical_xor(left_seen, right_seen))
        def _():
            only = jnp.where(left_seen, left, right)
            load_values(only, 0)
            for h in range(HEADS):
                acc[h] = merge(dot_t(qs[h], chip_keys(only)), vd[:CHIP], top, acc, h)

        return 0

    lax.fori_loop(0, len(PLAN), step, 0)
    events(TAIL)

    for h in range(HEADS):
        out[:, h * HDIM : (h + 1) * HDIM] = (acc[h, :, :HDIM] / acc[h, :, HDIM:]).astype(BF16)

    pair = pair_ref[me]
    new_keys = ROWS * STEPS
    keys = jnp.concatenate([kv[pair, 0], nkf[...].astype(BF16)], axis=0)
    vd[:TOK, :HDIM] = kv[pair, 1]
    vd[TOK : TOK + new_keys, :HDIM] = nvf[...].astype(BF16)
    values = vd[: TOK + new_keys, :]
    per = STEPS * HEADS

    def decode_last(g, _):
        rows = pl.ds(8 * g, 8)
        size = 8 * per
        scores = dot_t(dqs[rows].reshape(size, HDIM), keys) * FACTOR
        column = lax.broadcasted_iota(jnp.int32, (size, new_keys), 1)
        row = lax.broadcasted_iota(jnp.int32, (size, new_keys), 0) + g * size
        keep = jnp.logical_and(
            column // STEPS == row // per,
            lax.rem(column, STEPS) <= lax.rem(row // HEADS, STEPS),
        )
        fresh = jnp.where(keep, scores[:, TOK:], NEG)
        scores = jnp.concatenate([scores[:, :TOK], fresh], axis=1)
        before = dtop[rows].reshape(size, HDIM)
        peak = jnp.maximum(before, jnp.max(scores, axis=1, keepdims=True))
        p = jnp.exp2(scores - wide(peak, TOK + new_keys)).astype(BF16)
        total = wide(jnp.exp2(before - peak), 2 * HDIM) * dacc[rows].reshape(size, 2 * HDIM)
        total = total + jnp.dot(p, values, preferred_element_type=F32)
        dqf[rows] = (total[:, :HDIM] / total[:, HDIM:]).reshape(8, per, HDIM)
        return 0

    lax.fori_loop(0, 4, decode_last, 0)
    for h in range(HEADS):
        dout[:, :, h * HDIM : (h + 1) * HDIM] = dqf[:, pl.ds(h, STEPS, stride=HEADS), :].astype(BF16)
    for item, to in SENDS:
        remote(item, to).wait_send()
    for chip in CHIPS:
        twin(*chip).wait_send()


def per_device(*args):
    any_spec = pl.BlockSpec(memory_space=pl.ANY)
    smem = pl.BlockSpec(memory_space=pltpu.SMEM)
    vmem = pltpu.VMEM
    vspec = pl.BlockSpec(memory_space=pltpu.VMEM)
    per = STEPS * HEADS
    return pl.pallas_call(
        kernel,
        out_shape=(
            pltpu.VMEM((TOK, HEADS * HDIM), BF16),
            pltpu.VMEM((ROWS, STEPS, HEADS * HDIM), BF16),
        ),
        in_specs=[any_spec] * 8 + [smem, smem],
        out_specs=(vspec, vspec),
        scratch_shapes=[
            vmem((NINST, 2, TOK, HDIM), BF16),
            vmem((TOK, HEADS * HDIM), BF16),
            vmem((ROWS, STEPS, HEADS * HDIM), BF16),
            vmem((ROWS, STEPS, HDIM), BF16),
            vmem((ROWS, STEPS, HDIM), BF16),
            vmem((ROWS, CACHE, HDIM), BF16),
            vmem((ROWS, CACHE, HDIM), BF16),
            vmem((HEADS, TOK, HDIM), BF16),
            vmem((HEADS, TOK, 2 * HDIM), F32),
            vmem((HEADS, TOK, HDIM), F32),
            vmem((2 * CHIP, 2 * HDIM), BF16),
            vmem((ROWS, per, HDIM), F32),
            vmem((ROWS, per, HDIM), BF16),
            vmem((ROWS, per, 2 * HDIM), F32),
            vmem((ROWS, per, HDIM), F32),
            vmem((ROWS * STEPS, HDIM), F32),
            vmem((ROWS * STEPS, HDIM), F32),
            pltpu.SemaphoreType.DMA((len(SENDS),)),
            pltpu.SemaphoreType.DMA((NINST, 2)),
            pltpu.SemaphoreType.DMA((len(CHIPS),)),
            pltpu.SemaphoreType.DMA((NINST,)),
            pltpu.SemaphoreType.DMA((8,)),
            pltpu.SemaphoreType.DMA((4, 2)),
        ],
        compiler_params=pltpu.CompilerParams(
            collective_id=0, has_side_effects=True, vmem_limit_bytes=56 * 2**20
        ),
    )(*args)


def solution(mesh):
    return jax.shard_map(
        per_device,
        mesh=mesh,
        in_specs=(
            P("inst", "tp"),
            P("inst", "tp"),
            P("inst", "tp"),
            P("inst", None, "tp"),
            P("inst", None, "tp"),
            P("inst", None, "tp"),
            P("inst", None, "tp"),
            P("inst", None, "tp"),
            P("inst"),
            P(),
        ),
        out_specs=(P("inst", "tp"), P("inst", None, "tp")),
        check_vma=False,
    )
```

```python
import math

import jax
import jax.numpy as jnp
from jax import lax
from jax.experimental import pallas as pl
from jax.experimental.pallas import tpu as pltpu
from jax.sharding import PartitionSpec as P

MESH = pl.DeviceIdType.MESH
BF16 = jnp.bfloat16
F32 = jnp.float32

HDIM = 128
HEADS = 8
TOK = 256
ROWS = 32
CACHE = 256
STEPS = 4
NZ = 8
NINST = 32
CHIP = 2 * TOK
NEG = -1e30
FACTOR = HDIM**-0.5 * math.log2(math.e)

ROUTE = {
    ('A', -1, 0): (1, 0),
    ('A', 1, 0): (-1, 0),
    ('A', -1, 1): (1, 0),
    ('A', 1, 1): (-1, 0),
    ('B', -1, 0): (1, 0),
    ('B', 1, 1): (-1, 0),
    ('B', 1, 0): (0, 1),
    ('B', -1, 1): (0, 1),
    ('A', -2, 0): (1, 0),
    ('A', 2, 0): (-1, 0),
    ('A', -2, 1): (1, 0),
    ('A', 2, 1): (-1, 0),
    ('B', -2, 0): (1, 0),
    ('B', 2, 1): (-1, 0),
    ('B', 2, 0): (0, 1),
    ('B', -2, 1): (0, 1),
    ('A', -3, 0): (1, 0),
    ('A', 3, 0): (-1, 0),
    ('A', -3, 1): (1, 0),
    ('A', 3, 1): (-1, 0),
    ('B', -3, 0): (1, 0),
    ('B', 3, 1): (-1, 0),
    ('B', 3, 0): (0, 1),
    ('B', -3, 1): (0, 1),
    ('A', -4, 0): (1, 0),
    ('A', 4, 1): (-1, 0),
    ('B', 0, 0): (0, 1),
    ('B', 0, 1): (0, 1),
    ('B', -4, 0): (0, 1),
    ('B', 4, 1): (0, 1),
}

HEAD = [
    ([], 'dec'),
    ([('A', 1, 0), ('A', -1, 0), ('A', -1, 1), ('A', 1, 1)], 'own'),
    ([('B', 0, 1), ('B', 0, 0)], 'dec'),
]
PLAN = [
    ([('A', 2, 0), ('A', 2, 1), ('A', -2, 1), ('A', -2, 0)], [('A', -1)]),
    ([('B', 1, 1), ('B', -1, 1), ('B', -1, 0)], [('A', 2), ('A', 1)]),
    ([('A', -3, 1), ('B', 2, 0), ('B', 1, 0), ('A', 3, 0), ('A', 3, 1), ('A', -3, 0)], [('B', 0), ('B', -1)]),
    ([('B', -2, 1), ('B', -2, 0)], [('B', 1), ('A', -3)]),
    ([('B', 2, 1), ('A', -4, 0), ('A', 4, 1), ('B', -3, 1), ('B', -3, 0)], [('B', -2), ('A', -2)]),
    ([], [('B', -3), ('B', 2)]),
    ([('B', -4, 0), ('B', 4, 1), ('B', 3, 1), ('B', 3, 0)], [('A', 3), ('A', 4)]),
    ([], [('B', 3), ('B', 4)]),
]
TAIL = []


def forwards(item):
    col, d, part = item
    moves = []
    for (to_col, to_d, to_part), (dz, dy) in ROUTE.items():
        from_col = to_col if dy == 0 else "AB"["BA".index(to_col)]
        if (from_col, to_d + dz, to_part) == (col, d, part):
            moves.append((abs(to_d), dz, dy))
    return [(dz, dy) for _, dz, dy in sorted(moves)]


OWN = [("A", 0, 0), ("A", 0, 1)]
SENDS = [(item, to) for item in OWN + list(ROUTE) for to in forwards(item)]
CHIPS = [(col, d) for col in ("A", "B") for d in (-3, -2, -1, 0, 1, 2, 3, 4)]
PARTNERS = sorted({((way * dz) % NZ, dy) for dz, dy in ROUTE.values() for way in (1, -1)})
SEND_INDEX = {key: i for i, key in enumerate(SENDS)}


def kernel(
    q_hbm, k_hbm, v_hbm, dq_hbm, nk_hbm, nv_hbm, ck_hbm, cv_hbm, clen_ref, pair_ref,
    out, dout,
    kv, q, dq, nk, nv, ck, cv, qs, acc, top, vd, even, odd, dqf, dqs, dacc, dtop, nkf, nvf,
    send_sem, recv_sem, twin_send, twin_recv, local_sem, cache_sem,
):
    me = lax.axis_index("inst")
    core = lax.rem(me, 2)
    y = lax.rem(me // 2, 2)
    z = me // 4

    def slot(col, d):
        zz = lax.rem(z + (d + NZ), NZ)
        yy = y if col == "A" else 1 - y
        return 4 * zz + 2 * yy + core

    def device(dz, dy):
        return {"inst": 4 * lax.rem(z + dz + NZ, NZ) + 2 * (y if dy == 0 else 1 - y) + core}

    twin_device = {"inst": me + 1 - 2 * core}

    def remote(item, to):
        col, d, part = item
        place = slot(col, d)
        return pltpu.make_async_remote_copy(
            src_ref=kv.at[place, part],
            dst_ref=kv.at[place, part],
            send_sem=send_sem.at[SEND_INDEX[item, to]],
            recv_sem=recv_sem.at[place, part],
            device_id=device(*to),
            device_id_type=MESH,
        )

    def twin(col, d):
        place = slot(col, d)
        return pltpu.make_async_remote_copy(
            src_ref=kv.at[place],
            dst_ref=kv.at[place],
            send_sem=twin_send.at[CHIPS.index((col, d))],
            recv_sem=twin_recv.at[place],
            device_id=twin_device,
            device_id_type=MESH,
        )

    half = set()

    def arrived(place, part):
        pltpu.make_async_remote_copy(
            src_ref=kv.at[place, part],
            dst_ref=kv.at[place, part],
            send_sem=send_sem.at[0],
            recv_sem=recv_sem.at[place, part],
            device_id=twin_device,
            device_id_type=MESH,
        ).wait_recv()

    def events(items):
        for item in items:
            arrived(slot(item[0], item[1]), item[2])
            for to in forwards(item):
                remote(item, to).start()
            chip = (item[0], abs(item[1]) if abs(item[1]) == 4 else item[1])
            if chip in half:
                twin(*chip).start()
            half.add(chip)

    def twin_chip(col, d):
        place = slot(col, d) + 1 - 2 * core
        pltpu.make_async_remote_copy(
            src_ref=kv.at[place],
            dst_ref=kv.at[place],
            send_sem=twin_send.at[0],
            recv_sem=twin_recv.at[place],
            device_id=twin_device,
            device_id_type=MESH,
        ).wait_recv()

    own = [
        pltpu.make_async_copy(k_hbm, kv.at[me, 0], local_sem.at[0]),
        pltpu.make_async_copy(v_hbm, kv.at[me, 1], local_sem.at[1]),
    ]
    small = [
        pltpu.make_async_copy(dq_hbm, dq, local_sem.at[2]),
        pltpu.make_async_copy(nk_hbm, nk, local_sem.at[3]),
        pltpu.make_async_copy(nv_hbm, nv, local_sem.at[4]),
    ]
    queries = pltpu.make_async_copy(q_hbm, q, local_sem.at[5])

    def cache_copies(g):
        rows = pl.ds(8 * g, 8)
        return (
            pltpu.make_async_copy(ck_hbm.at[rows], ck.at[rows], cache_sem.at[g, 0]),
            pltpu.make_async_copy(cv_hbm.at[rows], cv.at[rows], cache_sem.at[g, 1]),
        )

    for copy in own + small:
        copy.start()
    for g in range(4):
        for copy in cache_copies(g):
            copy.start()
    queries.start()

    barrier = pltpu.get_barrier_semaphore()
    for to in PARTNERS:
        pl.semaphore_signal(barrier, inc=1, device_id=device(*to), device_id_type=MESH)
    pl.semaphore_signal(barrier, inc=1, device_id=twin_device, device_id_type=MESH)
    pl.semaphore_wait(barrier, len(PARTNERS) + 1)

    for part in (0, 1):
        own[part].wait()
        for to in forwards(OWN[part]):
            remote(OWN[part], to).start()
    twin("A", 0).start()

    for copy in small:
        copy.wait()
    for h in range(HEADS):
        dqf[:, pl.ds(h, STEPS, stride=HEADS), :] = dq[:, :, h * HDIM : (h + 1) * HDIM].astype(F32)
    dqs[...] = dqf[...].astype(BF16)
    for a in range(ROWS):
        nkf[a * STEPS : (a + 1) * STEPS, :] = nk[a].astype(F32)
        nvf[a * STEPS : (a + 1) * STEPS, :] = nv[a].astype(F32)
    vd[:, HDIM:] = jnp.ones((4 * CHIP, HDIM), BF16)

    def dot_t(a, b):
        return lax.dot_general(a, b, (((1,), (1,)), ((), ())), preferred_element_type=F32)

    def wide(x, width):
        return jnp.concatenate([x] * (width // HDIM), axis=1)

    ones = jnp.ones((CACHE, HDIM), BF16)

    def decode_rows(g):
        for part in (0, 1):
            for copy in cache_copies(2 * g + part):
                copy.wait()
        for u in range(16):
            a = 16 * g + u
            scores = dot_t(dqs[a], ck[a]) * FACTOR
            live = lax.broadcasted_iota(jnp.int32, scores.shape, 1) < clen_ref[a]
            scores = jnp.where(live, scores, NEG)
            peak = jnp.max(scores, axis=1, keepdims=True)
            p = jnp.exp2(scores - peak).astype(BF16)
            dtop[a] = jnp.broadcast_to(peak, (STEPS * HEADS, HDIM))
            dacc[a] = jnp.dot(
                p, jnp.concatenate([cv[a], ones], axis=1), preferred_element_type=F32
            )

    def chip_keys(chip):
        return kv[pl.ds(2 * chip, 2), 0].reshape(CHIP, HDIM)

    def load_values(chip, at):
        vd[at * CHIP : (at + 1) * CHIP, :HDIM] = kv[pl.ds(2 * chip, 2), 1].reshape(CHIP, HDIM)

    def own_chip():
        queries.wait()
        for h in range(HEADS):
            qs[h] = q[:, h * HDIM : (h + 1) * HDIM]
        twin_chip("A", 0)
        chip = me // 2
        load_values(chip, 0)
        for h in range(HEADS):
            scores = dot_t(qs[h], chip_keys(chip))
            key = lax.broadcasted_iota(jnp.int32, scores.shape, 1)
            row = lax.broadcasted_iota(jnp.int32, scores.shape, 0)
            scores = jnp.where(key <= row + TOK * core, scores, NEG)
            peak = jnp.max(scores, axis=1, keepdims=True) * FACTOR
            p = jnp.exp2(scores * FACTOR - peak).astype(BF16)
            top[h] = jnp.broadcast_to(peak, (TOK, HDIM))
            acc[h] = jnp.dot(p, vd[:CHIP], preferred_element_type=F32)

    done = 0
    for items, what in HEAD:
        events(items)
        if what == "dec":
            decode_rows(done)
            done += 1
        else:
            own_chip()

    def merge(scores, values, top_ref, acc_ref, index):
        before = top_ref[index]
        peak = jnp.maximum(before, jnp.max(scores, axis=1, keepdims=True) * FACTOR)
        top_ref[index] = peak
        p = jnp.exp2(scores * FACTOR - wide(peak, scores.shape[1])).astype(BF16)
        scale = jnp.exp2(before - peak)
        return wide(scale, 2 * HDIM) * acc_ref[index] + jnp.dot(
            p, values, preferred_element_type=F32
        )

    def chip_of(col, d):
        return 2 * lax.rem(z + d + NZ, NZ) + (y if col == "A" else 1 - y)

    def step(t, _):
        for i, (items, chips) in enumerate(PLAN):

            @pl.when(t == i)
            def _(items=items, chips=chips):
                events(items)
                for chip in chips:
                    twin_chip(*chip)

        mine = me // 2
        chips = []
        seen = []
        for k in range(max(len(c) for _, c in PLAN)):
            chip = mine
            for i, (_, listed) in enumerate(PLAN):
                if k < len(listed):
                    chip = jnp.where(t == i, chip_of(*listed[k]), chip)
            chips.append(chip)
            seen.append(chip < mine)
        for last in range(len(chips) - 1, 0, -1):
            for k in range(last):
                swap = jnp.logical_and(jnp.logical_not(seen[k]), seen[k + 1])
                chips[k], chips[k + 1] = (
                    jnp.where(swap, chips[k + 1], chips[k]),
                    jnp.where(swap, chips[k], chips[k + 1]),
                )
                seen[k], seen[k + 1] = (
                    jnp.logical_or(seen[k], seen[k + 1]),
                    jnp.logical_and(seen[k], seen[k + 1]),
                )
        count = sum(flag.astype(jnp.int32) for flag in seen)

        def attend(some):
            width = len(some) * CHIP
            for k, chip in enumerate(some):
                load_values(chip, k)

            def score(h):
                keys = jnp.concatenate([chip_keys(chip) for chip in some], axis=0)
                (even if h % 2 == 0 else odd)[:, :width] = dot_t(qs[h], keys)

            score(0)
            for h in range(HEADS):
                if h + 1 < HEADS:
                    score(h + 1)
                scores = (even if h % 2 == 0 else odd)[:, :width]
                acc[h] = merge(scores, vd[:width], top, acc, h)

        if len(chips) > 3:

            @pl.when(count == 4)
            def _():
                attend(chips[:4])

        @pl.when(jnp.logical_or(count == 2, count == 3))
        def _():
            attend(chips[:2])

        @pl.when(jnp.logical_or(count == 1, count == 3))
        def _():
            attend([jnp.where(count == 3, chips[min(2, len(chips) - 1)], chips[0])])

        return 0

    lax.fori_loop(0, len(PLAN), step, 0)
    events(TAIL)

    for h in range(HEADS):
        out[:, h * HDIM : (h + 1) * HDIM] = (acc[h, :, :HDIM] / acc[h, :, HDIM:]).astype(BF16)

    pair = pair_ref[me]
    new_keys = ROWS * STEPS
    keys = jnp.concatenate([kv[pair, 0], nkf[...].astype(BF16)], axis=0)
    vd[:TOK, :HDIM] = kv[pair, 1]
    vd[TOK : TOK + new_keys, :HDIM] = nvf[...].astype(BF16)
    values = vd[: TOK + new_keys, :]
    per = STEPS * HEADS

    size = 8 * per
    column = lax.broadcasted_iota(jnp.int32, (size, new_keys), 1)
    row = lax.broadcasted_iota(jnp.int32, (size, new_keys), 0)
    allowed = (column & (STEPS - 1)) <= ((row >> 3) & (STEPS - 1))
    behind = (column >> 2) - (row >> 5)

    def last_scores(g):
        return dot_t(dqs[8 * g : 8 * g + 8].reshape(size, HDIM), keys)

    def decode_last(g, scores):
        rows = slice(8 * g, 8 * g + 8)
        keep = jnp.logical_and(allowed, behind == 8 * g)
        scores = scores * FACTOR
        fresh = jnp.where(keep, scores[:, TOK:], NEG)
        scores = jnp.concatenate([scores[:, :TOK], fresh], axis=1)
        before = dtop[rows].reshape(size, HDIM)
        peak = jnp.maximum(before, jnp.max(scores, axis=1, keepdims=True))
        p = jnp.exp2(scores - wide(peak, TOK + new_keys)).astype(BF16)
        total = wide(jnp.exp2(before - peak), 2 * HDIM) * dacc[rows].reshape(size, 2 * HDIM)
        total = total + jnp.dot(p, values, preferred_element_type=F32)
        dqf[rows] = (total[:, :HDIM] / total[:, HDIM:]).reshape(8, per, HDIM)

    for g in range(ROWS // 8):
        decode_last(g, last_scores(g))
    for h in range(HEADS):
        dout[:, :, h * HDIM : (h + 1) * HDIM] = dqf[:, pl.ds(h, STEPS, stride=HEADS), :].astype(BF16)
    for item, to in SENDS:
        remote(item, to).wait_send()
    for chip in CHIPS:
        twin(*chip).wait_send()


def per_device(*args):
    any_spec = pl.BlockSpec(memory_space=pl.ANY)
    smem = pl.BlockSpec(memory_space=pltpu.SMEM)
    vmem = pltpu.VMEM
    vspec = pl.BlockSpec(memory_space=pltpu.VMEM)
    per = STEPS * HEADS
    return pl.pallas_call(
        kernel,
        out_shape=(
            pltpu.VMEM((TOK, HEADS * HDIM), BF16),
            pltpu.VMEM((ROWS, STEPS, HEADS * HDIM), BF16),
        ),
        in_specs=[any_spec] * 8 + [smem, smem],
        out_specs=(vspec, vspec),
        scratch_shapes=[
            vmem((NINST, 2, TOK, HDIM), BF16),
            vmem((TOK, HEADS * HDIM), BF16),
            vmem((ROWS, STEPS, HEADS * HDIM), BF16),
            vmem((ROWS, STEPS, HDIM), BF16),
            vmem((ROWS, STEPS, HDIM), BF16),
            vmem((ROWS, CACHE, HDIM), BF16),
            vmem((ROWS, CACHE, HDIM), BF16),
            vmem((HEADS, TOK, HDIM), BF16),
            vmem((HEADS, TOK, 2 * HDIM), F32),
            vmem((HEADS, TOK, HDIM), F32),
            vmem((4 * CHIP, 2 * HDIM), BF16),
            vmem((TOK, 4 * CHIP), F32),
            vmem((TOK, 4 * CHIP), F32),
            vmem((ROWS, per, HDIM), F32),
            vmem((ROWS, per, HDIM), BF16),
            vmem((ROWS, per, 2 * HDIM), F32),
            vmem((ROWS, per, HDIM), F32),
            vmem((ROWS * STEPS, HDIM), F32),
            vmem((ROWS * STEPS, HDIM), F32),
            pltpu.SemaphoreType.DMA((len(SENDS),)),
            pltpu.SemaphoreType.DMA((NINST, 2)),
            pltpu.SemaphoreType.DMA((len(CHIPS),)),
            pltpu.SemaphoreType.DMA((NINST,)),
            pltpu.SemaphoreType.DMA((8,)),
            pltpu.SemaphoreType.DMA((4, 2)),
        ],
        compiler_params=pltpu.CompilerParams(
            collective_id=0, has_side_effects=True, vmem_limit_bytes=56 * 2**20
        ),
    )(*args)


def solution(mesh):
    return jax.shard_map(
        per_device,
        mesh=mesh,
        in_specs=(
            P("inst", "tp"),
            P("inst", "tp"),
            P("inst", "tp"),
            P("inst", None, "tp"),
            P("inst", None, "tp"),
            P("inst", None, "tp"),
            P("inst", None, "tp"),
            P("inst", None, "tp"),
            P("inst"),
            P(),
        ),
        out_specs=(P("inst", "tp"), P("inst", None, "tp")),
        check_vma=False,
    )
```

```python
import math

import jax
import jax.numpy as jnp
from jax import lax
from jax.experimental import pallas as pl
from jax.experimental.pallas import tpu as pltpu
from jax.sharding import PartitionSpec as P

MESH = pl.DeviceIdType.MESH
BF16 = jnp.bfloat16
F32 = jnp.float32

HDIM = 128
HEADS = 8
TOK = 256
ROWS = 32
CACHE = 256
STEPS = 4
NZ = 8
NINST = 32
CHIP = 2 * TOK
NEG = -1e30
FACTOR = HDIM**-0.5 * math.log2(math.e)

ROUTE = {
    ('A', -1, 0): (1, 0),
    ('A', 1, 0): (-1, 0),
    ('A', -1, 1): (1, 0),
    ('A', 1, 1): (-1, 0),
    ('B', -1, 0): (1, 0),
    ('B', 1, 1): (-1, 0),
    ('B', 1, 0): (0, 1),
    ('B', -1, 1): (0, 1),
    ('A', -2, 0): (1, 0),
    ('A', 2, 0): (-1, 0),
    ('A', -2, 1): (1, 0),
    ('A', 2, 1): (-1, 0),
    ('B', -2, 0): (1, 0),
    ('B', 2, 1): (-1, 0),
    ('B', 2, 0): (0, 1),
    ('B', -2, 1): (0, 1),
    ('A', -3, 0): (1, 0),
    ('A', 3, 0): (-1, 0),
    ('A', -3, 1): (1, 0),
    ('A', 3, 1): (-1, 0),
    ('B', -3, 0): (1, 0),
    ('B', 3, 1): (-1, 0),
    ('B', 3, 0): (0, 1),
    ('B', -3, 1): (0, 1),
    ('A', -4, 0): (1, 0),
    ('A', 4, 1): (-1, 0),
    ('B', 0, 0): (0, 1),
    ('B', 0, 1): (0, 1),
    ('B', -4, 0): (0, 1),
    ('B', 4, 1): (0, 1),
}

HEAD = [
    ([], 'dec'),
    ([('A', 1, 0), ('A', -1, 0), ('A', -1, 1), ('A', 1, 1)], 'own'),
    ([('B', 0, 1), ('B', 0, 0)], 'dec'),
]
PLAN = [
    ([('A', 2, 0), ('A', 2, 1), ('A', -2, 1), ('A', -2, 0)], [('A', -1)]),
    ([('B', 1, 1), ('B', -1, 1), ('B', -1, 0)], [('A', 2), ('A', 1)]),
    ([('A', -3, 1), ('B', 2, 0), ('B', 1, 0), ('A', 3, 0), ('A', 3, 1), ('A', -3, 0)], [('B', 0), ('B', -1)]),
    ([('B', -2, 1), ('B', -2, 0)], [('B', 1), ('A', -3)]),
    ([('B', 2, 1), ('A', -4, 0), ('A', 4, 1), ('B', -3, 1), ('B', -3, 0)], [('B', -2), ('A', -2)]),
    ([], [('B', -3), ('B', 2)]),
    ([('B', -4, 0), ('B', 4, 1), ('B', 3, 1), ('B', 3, 0)], [('A', 3), ('A', 4)]),
    ([], [('B', 3), ('B', 4)]),
]
TAIL = []


def forwards(item):
    col, d, part = item
    moves = []
    for (to_col, to_d, to_part), (dz, dy) in ROUTE.items():
        from_col = to_col if dy == 0 else "AB"["BA".index(to_col)]
        if (from_col, to_d + dz, to_part) == (col, d, part):
            moves.append((abs(to_d), dz, dy))
    return [(dz, dy) for _, dz, dy in sorted(moves)]


OWN = [("A", 0, 0), ("A", 0, 1)]
SENDS = [(item, to) for item in OWN + list(ROUTE) for to in forwards(item)]
CHIPS = [(col, d) for col in ("A", "B") for d in (-3, -2, -1, 0, 1, 2, 3, 4)]
PARTNERS = sorted({((way * dz) % NZ, dy) for dz, dy in ROUTE.values() for way in (1, -1)})
SEND_INDEX = {key: i for i, key in enumerate(SENDS)}


def kernel(
    q_hbm, k_hbm, v_hbm, dq_hbm, nk_hbm, nv_hbm, ck_hbm, cv_hbm, clen_ref, pair_ref,
    out, dout,
    kv, q, dq, nk, nv, ck, cv, qs, acc, top, vd, even, odd, dqf, dqs, dacc, dtop, nkf, nvf,
    send_sem, recv_sem, twin_send, twin_recv, local_sem, cache_sem,
):
    me = lax.axis_index("inst")
    core = lax.rem(me, 2)
    y = lax.rem(me // 2, 2)
    z = me // 4

    def slot(col, d):
        zz = lax.rem(z + (d + NZ), NZ)
        yy = y if col == "A" else 1 - y
        return 4 * zz + 2 * yy + core

    def device(dz, dy):
        return {"inst": 4 * lax.rem(z + dz + NZ, NZ) + 2 * (y if dy == 0 else 1 - y) + core}

    twin_device = {"inst": me + 1 - 2 * core}

    def remote(item, to):
        col, d, part = item
        place = slot(col, d)
        return pltpu.make_async_remote_copy(
            src_ref=kv.at[place, part],
            dst_ref=kv.at[place, part],
            send_sem=send_sem.at[SEND_INDEX[item, to]],
            recv_sem=recv_sem.at[place, part],
            device_id=device(*to),
            device_id_type=MESH,
        )

    def twin(col, d):
        place = slot(col, d)
        return pltpu.make_async_remote_copy(
            src_ref=kv.at[place],
            dst_ref=kv.at[place],
            send_sem=twin_send.at[CHIPS.index((col, d))],
            recv_sem=twin_recv.at[place],
            device_id=twin_device,
            device_id_type=MESH,
        )

    half = set()

    def arrived(place, part):
        pltpu.make_async_remote_copy(
            src_ref=kv.at[place, part],
            dst_ref=kv.at[place, part],
            send_sem=send_sem.at[0],
            recv_sem=recv_sem.at[place, part],
            device_id=twin_device,
            device_id_type=MESH,
        ).wait_recv()

    def events(items):
        for item in items:
            arrived(slot(item[0], item[1]), item[2])
            for to in forwards(item):
                remote(item, to).start()
            chip = (item[0], abs(item[1]) if abs(item[1]) == 4 else item[1])
            if chip in half:
                twin(*chip).start()
            half.add(chip)

    def twin_chip(col, d):
        place = slot(col, d) + 1 - 2 * core
        pltpu.make_async_remote_copy(
            src_ref=kv.at[place],
            dst_ref=kv.at[place],
            send_sem=twin_send.at[0],
            recv_sem=twin_recv.at[place],
            device_id=twin_device,
            device_id_type=MESH,
        ).wait_recv()

    own = [
        pltpu.make_async_copy(k_hbm, kv.at[me, 0], local_sem.at[0]),
        pltpu.make_async_copy(v_hbm, kv.at[me, 1], local_sem.at[1]),
    ]
    small = [
        pltpu.make_async_copy(dq_hbm, dq, local_sem.at[2]),
        pltpu.make_async_copy(nk_hbm, nk, local_sem.at[3]),
        pltpu.make_async_copy(nv_hbm, nv, local_sem.at[4]),
    ]
    queries = pltpu.make_async_copy(q_hbm, q, local_sem.at[5])

    def cache_copies(g):
        rows = pl.ds(8 * g, 8)
        return (
            pltpu.make_async_copy(ck_hbm.at[rows], ck.at[rows], cache_sem.at[g, 0]),
            pltpu.make_async_copy(cv_hbm.at[rows], cv.at[rows], cache_sem.at[g, 1]),
        )

    for copy in own + small:
        copy.start()
    for g in range(4):
        for copy in cache_copies(g):
            copy.start()
    queries.start()

    barrier = pltpu.get_barrier_semaphore()
    for to in PARTNERS:
        pl.semaphore_signal(barrier, inc=1, device_id=device(*to), device_id_type=MESH)
    pl.semaphore_signal(barrier, inc=1, device_id=twin_device, device_id_type=MESH)
    pl.semaphore_wait(barrier, len(PARTNERS) + 1)

    for part in (0, 1):
        own[part].wait()
        for to in forwards(OWN[part]):
            remote(OWN[part], to).start()
    twin("A", 0).start()

    for copy in small:
        copy.wait()
    for h in range(HEADS):
        dqf[:, pl.ds(h, STEPS, stride=HEADS), :] = dq[:, :, h * HDIM : (h + 1) * HDIM].astype(F32)
    dqs[...] = dqf[...].astype(BF16)
    for a in range(ROWS):
        nkf[a * STEPS : (a + 1) * STEPS, :] = nk[a].astype(F32)
        nvf[a * STEPS : (a + 1) * STEPS, :] = nv[a].astype(F32)
    vd[:, HDIM:] = jnp.ones((2 * CHIP, HDIM), BF16)

    def dot_t(a, b):
        return lax.dot_general(a, b, (((1,), (1,)), ((), ())), preferred_element_type=F32)

    def wide(x, width):
        return jnp.concatenate([x] * (width // HDIM), axis=1)

    ones = jnp.ones((CACHE, HDIM), BF16)

    def decode_rows(g):
        for part in (0, 1):
            for copy in cache_copies(2 * g + part):
                copy.wait()
        for u in range(16):
            a = 16 * g + u
            scores = dot_t(dqs[a], ck[a]) * FACTOR
            live = lax.broadcasted_iota(jnp.int32, scores.shape, 1) < clen_ref[a]
            scores = jnp.where(live, scores, NEG)
            peak = jnp.max(scores, axis=1, keepdims=True)
            p = jnp.exp2(scores - peak).astype(BF16)
            dtop[a] = jnp.broadcast_to(peak, (STEPS * HEADS, HDIM))
            dacc[a] = jnp.dot(
                p, jnp.concatenate([cv[a], ones], axis=1), preferred_element_type=F32
            )

    def chip_keys(chip):
        return kv[pl.ds(2 * chip, 2), 0].reshape(CHIP, HDIM)

    def load_values(chip, at):
        vd[at * CHIP : (at + 1) * CHIP, :HDIM] = kv[pl.ds(2 * chip, 2), 1].reshape(CHIP, HDIM)

    def own_chip():
        queries.wait()
        for h in range(HEADS):
            qs[h] = q[:, h * HDIM : (h + 1) * HDIM]
        twin_chip("A", 0)
        chip = me // 2
        load_values(chip, 0)

        def own_scores(h):
            (even if h % 2 == 0 else odd)[:, :CHIP] = dot_t(qs[h], chip_keys(chip))

        own_scores(0)
        for h in range(HEADS):
            if h + 1 < HEADS:
                own_scores(h + 1)
            scores = (even if h % 2 == 0 else odd)[:, :CHIP]
            key = lax.broadcasted_iota(jnp.int32, scores.shape, 1)
            row = lax.broadcasted_iota(jnp.int32, scores.shape, 0)
            scores = jnp.where(key <= row + TOK * core, scores, NEG)
            peak = jnp.max(scores, axis=1, keepdims=True) * FACTOR
            p = jnp.exp2(scores * FACTOR - peak).astype(BF16)
            top[h] = jnp.broadcast_to(peak, (TOK, HDIM))
            acc[h] = jnp.dot(p, vd[:CHIP], preferred_element_type=F32)

    done = 0
    for items, what in HEAD:
        events(items)
        if what == "dec":
            decode_rows(done)
            done += 1
        else:
            own_chip()

    def merge(scores, values, top_ref, acc_ref, index):
        before = top_ref[index]
        peak = jnp.maximum(before, jnp.max(scores, axis=1, keepdims=True) * FACTOR)
        top_ref[index] = peak
        p = jnp.exp2(scores * FACTOR - wide(peak, scores.shape[1])).astype(BF16)
        scale = jnp.exp2(before - peak)
        return wide(scale, 2 * HDIM) * acc_ref[index] + jnp.dot(
            p, values, preferred_element_type=F32
        )

    def chip_of(col, d):
        return 2 * lax.rem(z + d + NZ, NZ) + (y if col == "A" else 1 - y)

    def step(t, _):
        for i, (items, chips) in enumerate(PLAN):

            @pl.when(t == i)
            def _(items=items, chips=chips):
                events(items)
                for chip in chips:
                    twin_chip(*chip)

        mine = me // 2
        chips = []
        seen = []
        for k in range(max(len(c) for _, c in PLAN)):
            chip = mine
            for i, (_, listed) in enumerate(PLAN):
                if k < len(listed):
                    chip = jnp.where(t == i, chip_of(*listed[k]), chip)
            chips.append(chip)
            seen.append(chip < mine)
        for last in range(len(chips) - 1, 0, -1):
            for k in range(last):
                swap = jnp.logical_and(jnp.logical_not(seen[k]), seen[k + 1])
                chips[k], chips[k + 1] = (
                    jnp.where(swap, chips[k + 1], chips[k]),
                    jnp.where(swap, chips[k], chips[k + 1]),
                )
                seen[k], seen[k + 1] = (
                    jnp.logical_or(seen[k], seen[k + 1]),
                    jnp.logical_and(seen[k], seen[k + 1]),
                )
        count = sum(flag.astype(jnp.int32) for flag in seen)

        def attend(some):
            width = len(some) * CHIP
            for k, chip in enumerate(some):
                load_values(chip, k)

            def score(h):
                keys = jnp.concatenate([chip_keys(chip) for chip in some], axis=0)
                (even if h % 2 == 0 else odd)[:, :width] = dot_t(qs[h], keys)

            score(0)
            for h in range(HEADS):
                if h + 1 < HEADS:
                    score(h + 1)
                scores = (even if h % 2 == 0 else odd)[:, :width]
                acc[h] = merge(scores, vd[:width], top, acc, h)

        if len(chips) > 3:

            @pl.when(count == 4)
            def _():
                attend(chips[:4])

        @pl.when(jnp.logical_or(count == 2, count == 3))
        def _():
            attend(chips[:2])

        @pl.when(jnp.logical_or(count == 1, count == 3))
        def _():
            attend([jnp.where(count == 3, chips[min(2, len(chips) - 1)], chips[0])])

        return 0

    lax.fori_loop(0, len(PLAN), step, 0)
    events(TAIL)

    for h in range(HEADS):
        out[:, h * HDIM : (h + 1) * HDIM] = (acc[h, :, :HDIM] / acc[h, :, HDIM:]).astype(BF16)

    pair = pair_ref[me]
    new_keys = ROWS * STEPS
    keys = jnp.concatenate([kv[pair, 0], nkf[...].astype(BF16)], axis=0)
    vd[:TOK, :HDIM] = kv[pair, 1]
    vd[TOK : TOK + new_keys, :HDIM] = nvf[...].astype(BF16)
    values = vd[: TOK + new_keys, :]
    per = STEPS * HEADS

    size = 8 * per
    column = lax.broadcasted_iota(jnp.int32, (size, new_keys), 1)
    row = lax.broadcasted_iota(jnp.int32, (size, new_keys), 0)
    allowed = (column & (STEPS - 1)) <= ((row >> 3) & (STEPS - 1))
    behind = (column >> 2) - (row >> 5)

    def last_scores(g):
        return dot_t(dqs[8 * g : 8 * g + 8].reshape(size, HDIM), keys)

    def decode_last(g, scores):
        rows = slice(8 * g, 8 * g + 8)
        keep = jnp.logical_and(allowed, behind == 8 * g)
        scores = scores * FACTOR
        fresh = jnp.where(keep, scores[:, TOK:], NEG)
        scores = jnp.concatenate([scores[:, :TOK], fresh], axis=1)
        before = dtop[rows].reshape(size, HDIM)
        peak = jnp.maximum(before, jnp.max(scores, axis=1, keepdims=True))
        p = jnp.exp2(scores - wide(peak, TOK + new_keys)).astype(BF16)
        total = wide(jnp.exp2(before - peak), 2 * HDIM) * dacc[rows].reshape(size, 2 * HDIM)
        total = total + jnp.dot(p, values, preferred_element_type=F32)
        dqf[rows] = (total[:, :HDIM] / total[:, HDIM:]).reshape(8, per, HDIM)

    width = TOK + new_keys
    even[:, :width] = last_scores(0)
    for g in range(ROWS // 8):
        if g + 1 < ROWS // 8:
            (odd if g % 2 == 0 else even)[:, :width] = last_scores(g + 1)
        decode_last(g, (even if g % 2 == 0 else odd)[:, :width])
    for h in range(HEADS):
        dout[:, :, h * HDIM : (h + 1) * HDIM] = dqf[:, pl.ds(h, STEPS, stride=HEADS), :].astype(BF16)
    for item, to in SENDS:
        remote(item, to).wait_send()
    for chip in CHIPS:
        twin(*chip).wait_send()


def per_device(*args):
    any_spec = pl.BlockSpec(memory_space=pl.ANY)
    smem = pl.BlockSpec(memory_space=pltpu.SMEM)
    vmem = pltpu.VMEM
    vspec = pl.BlockSpec(memory_space=pltpu.VMEM)
    per = STEPS * HEADS
    return pl.pallas_call(
        kernel,
        out_shape=(
            pltpu.VMEM((TOK, HEADS * HDIM), BF16),
            pltpu.VMEM((ROWS, STEPS, HEADS * HDIM), BF16),
        ),
        in_specs=[any_spec] * 8 + [smem, smem],
        out_specs=(vspec, vspec),
        scratch_shapes=[
            vmem((NINST, 2, TOK, HDIM), BF16),
            vmem((TOK, HEADS * HDIM), BF16),
            vmem((ROWS, STEPS, HEADS * HDIM), BF16),
            vmem((ROWS, STEPS, HDIM), BF16),
            vmem((ROWS, STEPS, HDIM), BF16),
            vmem((ROWS, CACHE, HDIM), BF16),
            vmem((ROWS, CACHE, HDIM), BF16),
            vmem((HEADS, TOK, HDIM), BF16),
            vmem((HEADS, TOK, 2 * HDIM), F32),
            vmem((HEADS, TOK, HDIM), F32),
            vmem((2 * CHIP, 2 * HDIM), BF16),
            vmem((TOK, 2 * CHIP), F32),
            vmem((TOK, 2 * CHIP), F32),
            vmem((ROWS, per, HDIM), F32),
            vmem((ROWS, per, HDIM), BF16),
            vmem((ROWS, per, 2 * HDIM), F32),
            vmem((ROWS, per, HDIM), F32),
            vmem((ROWS * STEPS, HDIM), F32),
            vmem((ROWS * STEPS, HDIM), F32),
            pltpu.SemaphoreType.DMA((len(SENDS),)),
            pltpu.SemaphoreType.DMA((NINST, 2)),
            pltpu.SemaphoreType.DMA((len(CHIPS),)),
            pltpu.SemaphoreType.DMA((NINST,)),
            pltpu.SemaphoreType.DMA((8,)),
            pltpu.SemaphoreType.DMA((4, 2)),
        ],
        compiler_params=pltpu.CompilerParams(
            collective_id=0, has_side_effects=True, vmem_limit_bytes=56 * 2**20
        ),
    )(*args)


def solution(mesh):
    return jax.shard_map(
        per_device,
        mesh=mesh,
        in_specs=(
            P("inst", "tp"),
            P("inst", "tp"),
            P("inst", "tp"),
            P("inst", None, "tp"),
            P("inst", None, "tp"),
            P("inst", None, "tp"),
            P("inst", None, "tp"),
            P("inst", None, "tp"),
            P("inst"),
            P(),
        ),
        out_specs=(P("inst", "tp"), P("inst", None, "tp")),
        check_vma=False,
    )
```

```python
import math

import jax
import jax.numpy as jnp
from jax import lax
from jax.experimental import pallas as pl
from jax.experimental.pallas import tpu as pltpu
from jax.sharding import PartitionSpec as P

MESH = pl.DeviceIdType.MESH
BF16 = jnp.bfloat16
F32 = jnp.float32

HDIM = 128
HEADS = 8
TOK = 256
ROWS = 32
CACHE = 256
STEPS = 4
NZ = 8
NINST = 32
CHIP = 2 * TOK
NEG = -1e30
FACTOR = HDIM**-0.5 * math.log2(math.e)

ROUTE = {
    ('A', -1, 0): (1, 0),
    ('A', 1, 0): (-1, 0),
    ('A', -1, 1): (1, 0),
    ('A', 1, 1): (-1, 0),
    ('B', -1, 0): (1, 0),
    ('B', 1, 1): (-1, 0),
    ('B', 1, 0): (0, 1),
    ('B', -1, 1): (0, 1),
    ('A', -2, 0): (1, 0),
    ('A', 2, 0): (-1, 0),
    ('A', -2, 1): (1, 0),
    ('A', 2, 1): (-1, 0),
    ('B', -2, 0): (1, 0),
    ('B', 2, 1): (-1, 0),
    ('B', 2, 0): (0, 1),
    ('B', -2, 1): (0, 1),
    ('A', -3, 0): (1, 0),
    ('A', 3, 0): (-1, 0),
    ('A', -3, 1): (1, 0),
    ('A', 3, 1): (-1, 0),
    ('B', -3, 0): (1, 0),
    ('B', 3, 1): (-1, 0),
    ('B', 3, 0): (0, 1),
    ('B', -3, 1): (0, 1),
    ('A', -4, 0): (1, 0),
    ('A', 4, 1): (-1, 0),
    ('B', 0, 0): (0, 1),
    ('B', 0, 1): (0, 1),
    ('B', -4, 0): (0, 1),
    ('B', 4, 1): (0, 1),
}

HEAD = [
    ([], 'dec'),
    ([('A', 1, 0), ('A', -1, 0), ('A', -1, 1), ('A', 1, 1)], 'own'),
    ([('B', 0, 1), ('B', 0, 0)], 'dec'),
]
PLAN = [
    ([('A', 2, 0), ('A', 2, 1), ('A', -2, 1), ('A', -2, 0)], [('A', -1)]),
    ([('B', 1, 1), ('B', -1, 1), ('B', -1, 0)], [('A', 2), ('A', 1)]),
    ([('A', -3, 1), ('B', 2, 0), ('B', 1, 0), ('A', 3, 0), ('A', 3, 1), ('A', -3, 0)], [('B', 0), ('B', -1)]),
    ([('B', -2, 1), ('B', -2, 0)], [('B', 1), ('A', -3)]),
    ([('B', 2, 1), ('A', -4, 0), ('A', 4, 1), ('B', -3, 1), ('B', -3, 0)], [('B', -2), ('A', -2)]),
    ([], [('B', -3), ('B', 2)]),
    ([('B', -4, 0), ('B', 4, 1), ('B', 3, 1), ('B', 3, 0)], [('A', 3), ('A', 4)]),
    ([], [('B', 3), ('B', 4)]),
]
TAIL = []


def forwards(item):
    col, d, part = item
    moves = []
    for (to_col, to_d, to_part), (dz, dy) in ROUTE.items():
        from_col = to_col if dy == 0 else "AB"["BA".index(to_col)]
        if (from_col, to_d + dz, to_part) == (col, d, part):
            moves.append((abs(to_d), dz, dy))
    return [(dz, dy) for _, dz, dy in sorted(moves)]


OWN = [("A", 0, 0), ("A", 0, 1)]
SENDS = [(item, to) for item in OWN + list(ROUTE) for to in forwards(item)]
CHIPS = [(col, d) for col in ("A", "B") for d in (-3, -2, -1, 0, 1, 2, 3, 4)]
PARTNERS = sorted({((way * dz) % NZ, dy) for dz, dy in ROUTE.values() for way in (1, -1)})
SEND_INDEX = {key: i for i, key in enumerate(SENDS)}


def kernel(
    q_hbm, k_hbm, v_hbm, dq_hbm, nk_hbm, nv_hbm, ck_hbm, cv_hbm, clen_ref, pair_ref,
    out, dout,
    kv, q, dq, nk, nv, ck, cv, qs, acc, top, vd, even, odd, dqf, dqs, dacc, dtop, nkf, nvf,
    send_sem, recv_sem, twin_send, twin_recv, local_sem, cache_sem,
):
    me = lax.axis_index("inst")
    core = lax.rem(me, 2)
    y = lax.rem(me // 2, 2)
    z = me // 4

    def slot(col, d):
        zz = lax.rem(z + (d + NZ), NZ)
        yy = y if col == "A" else 1 - y
        return 4 * zz + 2 * yy + core

    def device(dz, dy):
        return {"inst": 4 * lax.rem(z + dz + NZ, NZ) + 2 * (y if dy == 0 else 1 - y) + core}

    twin_device = {"inst": me + 1 - 2 * core}

    def remote(item, to):
        col, d, part = item
        place = slot(col, d)
        return pltpu.make_async_remote_copy(
            src_ref=kv.at[place, part],
            dst_ref=kv.at[place, part],
            send_sem=send_sem.at[SEND_INDEX[item, to]],
            recv_sem=recv_sem.at[place, part],
            device_id=device(*to),
            device_id_type=MESH,
        )

    def twin(col, d):
        place = slot(col, d)
        return pltpu.make_async_remote_copy(
            src_ref=kv.at[place],
            dst_ref=kv.at[place],
            send_sem=twin_send.at[CHIPS.index((col, d))],
            recv_sem=twin_recv.at[place],
            device_id=twin_device,
            device_id_type=MESH,
        )

    half = set()

    def arrived(place, part):
        pltpu.make_async_remote_copy(
            src_ref=kv.at[place, part],
            dst_ref=kv.at[place, part],
            send_sem=send_sem.at[0],
            recv_sem=recv_sem.at[place, part],
            device_id=twin_device,
            device_id_type=MESH,
        ).wait_recv()

    def events(items):
        for item in items:
            arrived(slot(item[0], item[1]), item[2])
            for to in forwards(item):
                remote(item, to).start()
            chip = (item[0], abs(item[1]) if abs(item[1]) == 4 else item[1])
            if chip in half:
                twin(*chip).start()
            half.add(chip)

    def twin_chip(col, d):
        place = slot(col, d) + 1 - 2 * core
        pltpu.make_async_remote_copy(
            src_ref=kv.at[place],
            dst_ref=kv.at[place],
            send_sem=twin_send.at[0],
            recv_sem=twin_recv.at[place],
            device_id=twin_device,
            device_id_type=MESH,
        ).wait_recv()

    own = [
        pltpu.make_async_copy(k_hbm, kv.at[me, 0], local_sem.at[0]),
        pltpu.make_async_copy(v_hbm, kv.at[me, 1], local_sem.at[1]),
    ]
    small = [
        pltpu.make_async_copy(dq_hbm, dq, local_sem.at[2]),
        pltpu.make_async_copy(nk_hbm, nk, local_sem.at[3]),
        pltpu.make_async_copy(nv_hbm, nv, local_sem.at[4]),
    ]
    queries = pltpu.make_async_copy(q_hbm, q, local_sem.at[5])

    def cache_copies(g):
        rows = pl.ds(8 * g, 8)
        return (
            pltpu.make_async_copy(ck_hbm.at[rows], ck.at[rows], cache_sem.at[g, 0]),
            pltpu.make_async_copy(cv_hbm.at[rows], cv.at[rows], cache_sem.at[g, 1]),
        )

    for copy in own + small:
        copy.start()
    for g in range(4):
        for copy in cache_copies(g):
            copy.start()
    queries.start()

    barrier = pltpu.get_barrier_semaphore()
    for to in PARTNERS:
        pl.semaphore_signal(barrier, inc=1, device_id=device(*to), device_id_type=MESH)
    pl.semaphore_signal(barrier, inc=1, device_id=twin_device, device_id_type=MESH)
    vd[:, HDIM:] = jnp.ones((2 * CHIP, HDIM), BF16)
    pl.semaphore_wait(barrier, len(PARTNERS) + 1)

    for part in (0, 1):
        own[part].wait()
        for to in forwards(OWN[part]):
            remote(OWN[part], to).start()
    twin("A", 0).start()

    for copy in small:
        copy.wait()
    for h in range(HEADS):
        dqf[:, pl.ds(h, STEPS, stride=HEADS), :] = dq[:, :, h * HDIM : (h + 1) * HDIM].astype(F32)
    dqs[...] = dqf[...].astype(BF16)
    for a in range(ROWS):
        nkf[a * STEPS : (a + 1) * STEPS, :] = nk[a].astype(F32)
        nvf[a * STEPS : (a + 1) * STEPS, :] = nv[a].astype(F32)

    def dot_t(a, b):
        return lax.dot_general(a, b, (((1,), (1,)), ((), ())), preferred_element_type=F32)

    def wide(x, width):
        return jnp.concatenate([x] * (width // HDIM), axis=1)

    ones = jnp.ones((CACHE, HDIM), BF16)

    def decode_rows(g):
        for part in (0, 1):
            for copy in cache_copies(2 * g + part):
                copy.wait()
        for u in range(16):
            a = 16 * g + u
            scores = dot_t(dqs[a], ck[a]) * FACTOR
            live = lax.broadcasted_iota(jnp.int32, scores.shape, 1) < clen_ref[a]
            scores = jnp.where(live, scores, NEG)
            peak = jnp.max(scores, axis=1, keepdims=True)
            p = jnp.exp2(scores - peak).astype(BF16)
            dtop[a] = jnp.broadcast_to(peak, (STEPS * HEADS, HDIM))
            dacc[a] = jnp.dot(
                p, jnp.concatenate([cv[a], ones], axis=1), preferred_element_type=F32
            )

    def chip_keys(chip):
        return kv[pl.ds(2 * chip, 2), 0].reshape(CHIP, HDIM)

    def load_values(chip, at):
        vd[at * CHIP : (at + 1) * CHIP, :HDIM] = kv[pl.ds(2 * chip, 2), 1].reshape(CHIP, HDIM)

    def own_chip():
        queries.wait()
        for h in range(HEADS):
            qs[h] = q[:, h * HDIM : (h + 1) * HDIM]
        twin_chip("A", 0)
        chip = me // 2
        load_values(chip, 0)

        def own_scores(h):
            (even if h % 2 == 0 else odd)[:, :CHIP] = dot_t(qs[h], chip_keys(chip))

        own_scores(0)
        for h in range(HEADS):
            if h + 1 < HEADS:
                own_scores(h + 1)
            scores = (even if h % 2 == 0 else odd)[:, :CHIP]
            key = lax.broadcasted_iota(jnp.int32, scores.shape, 1)
            row = lax.broadcasted_iota(jnp.int32, scores.shape, 0)
            scores = jnp.where(key <= row + TOK * core, scores, NEG)
            peak = jnp.max(scores, axis=1, keepdims=True) * FACTOR
            p = jnp.exp2(scores * FACTOR - peak).astype(BF16)
            top[h] = jnp.broadcast_to(peak, (TOK, HDIM))
            acc[h] = jnp.dot(p, vd[:CHIP], preferred_element_type=F32)

    done = 0
    for items, what in HEAD:
        events(items)
        if what == "dec":
            decode_rows(done)
            done += 1
        else:
            own_chip()

    def merge(scores, values, top_ref, acc_ref, index):
        before = top_ref[index]
        peak = jnp.maximum(before, jnp.max(scores, axis=1, keepdims=True) * FACTOR)
        top_ref[index] = peak
        p = jnp.exp2(scores * FACTOR - wide(peak, scores.shape[1])).astype(BF16)
        scale = jnp.exp2(before - peak)
        return wide(scale, 2 * HDIM) * acc_ref[index] + jnp.dot(
            p, values, preferred_element_type=F32
        )

    def chip_of(col, d):
        return 2 * lax.rem(z + d + NZ, NZ) + (y if col == "A" else 1 - y)

    def step(t, _):
        for i, (items, chips) in enumerate(PLAN):

            @pl.when(t == i)
            def _(items=items, chips=chips):
                events(items)
                for chip in chips:
                    twin_chip(*chip)

        mine = me // 2
        chips = []
        seen = []
        for k in range(max(len(c) for _, c in PLAN)):
            chip = mine
            for i, (_, listed) in enumerate(PLAN):
                if k < len(listed):
                    chip = jnp.where(t == i, chip_of(*listed[k]), chip)
            chips.append(chip)
            seen.append(chip < mine)
        for last in range(len(chips) - 1, 0, -1):
            for k in range(last):
                swap = jnp.logical_and(jnp.logical_not(seen[k]), seen[k + 1])
                chips[k], chips[k + 1] = (
                    jnp.where(swap, chips[k + 1], chips[k]),
                    jnp.where(swap, chips[k], chips[k + 1]),
                )
                seen[k], seen[k + 1] = (
                    jnp.logical_or(seen[k], seen[k + 1]),
                    jnp.logical_and(seen[k], seen[k + 1]),
                )
        count = sum(flag.astype(jnp.int32) for flag in seen)

        def attend(some):
            width = len(some) * CHIP
            for k, chip in enumerate(some):
                load_values(chip, k)

            def score(h):
                keys = jnp.concatenate([chip_keys(chip) for chip in some], axis=0)
                (even if h % 2 == 0 else odd)[:, :width] = dot_t(qs[h], keys)

            score(0)
            for h in range(HEADS):
                if h + 1 < HEADS:
                    score(h + 1)
                scores = (even if h % 2 == 0 else odd)[:, :width]
                acc[h] = merge(scores, vd[:width], top, acc, h)

        if len(chips) > 3:

            @pl.when(count == 4)
            def _():
                attend(chips[:4])

        @pl.when(jnp.logical_or(count == 2, count == 3))
        def _():
            attend(chips[:2])

        @pl.when(jnp.logical_or(count == 1, count == 3))
        def _():
            attend([jnp.where(count == 3, chips[min(2, len(chips) - 1)], chips[0])])

        return 0

    lax.fori_loop(0, len(PLAN), step, 0)
    events(TAIL)

    for h in range(HEADS):
        out[:, h * HDIM : (h + 1) * HDIM] = (acc[h, :, :HDIM] / acc[h, :, HDIM:]).astype(BF16)

    pair = pair_ref[me]
    new_keys = ROWS * STEPS
    keys = jnp.concatenate([kv[pair, 0], nkf[...].astype(BF16)], axis=0)
    vd[:TOK, :HDIM] = kv[pair, 1]
    vd[TOK : TOK + new_keys, :HDIM] = nvf[...].astype(BF16)
    values = vd[: TOK + new_keys, :]
    per = STEPS * HEADS

    size = 8 * per
    column = lax.broadcasted_iota(jnp.int32, (size, new_keys), 1)
    row = lax.broadcasted_iota(jnp.int32, (size, new_keys), 0)
    allowed = (column & (STEPS - 1)) <= ((row >> 3) & (STEPS - 1))
    behind = (column >> 2) - (row >> 5)

    def last_scores(g):
        return dot_t(dqs[8 * g : 8 * g + 8].reshape(size, HDIM), keys)

    def decode_last(g, scores):
        rows = slice(8 * g, 8 * g + 8)
        keep = jnp.logical_and(allowed, behind == 8 * g)
        scores = scores * FACTOR
        fresh = jnp.where(keep, scores[:, TOK:], NEG)
        scores = jnp.concatenate([scores[:, :TOK], fresh], axis=1)
        before = dtop[rows].reshape(size, HDIM)
        peak = jnp.maximum(before, jnp.max(scores, axis=1, keepdims=True))
        p = jnp.exp2(scores - wide(peak, TOK + new_keys)).astype(BF16)
        total = wide(jnp.exp2(before - peak), 2 * HDIM) * dacc[rows].reshape(size, 2 * HDIM)
        total = total + jnp.dot(p, values, preferred_element_type=F32)
        dqf[rows] = (total[:, :HDIM] / total[:, HDIM:]).reshape(8, per, HDIM)

    width = TOK + new_keys
    even[:, :width] = last_scores(0)
    for g in range(ROWS // 8):
        if g + 1 < ROWS // 8:
            (odd if g % 2 == 0 else even)[:, :width] = last_scores(g + 1)
        decode_last(g, (even if g % 2 == 0 else odd)[:, :width])
    for h in range(HEADS):
        dout[:, :, h * HDIM : (h + 1) * HDIM] = dqf[:, pl.ds(h, STEPS, stride=HEADS), :].astype(BF16)
    for item, to in SENDS:
        remote(item, to).wait_send()
    for chip in CHIPS:
        twin(*chip).wait_send()


def per_device(*args):
    any_spec = pl.BlockSpec(memory_space=pl.ANY)
    smem = pl.BlockSpec(memory_space=pltpu.SMEM)
    vmem = pltpu.VMEM
    vspec = pl.BlockSpec(memory_space=pltpu.VMEM)
    per = STEPS * HEADS
    return pl.pallas_call(
        kernel,
        out_shape=(
            pltpu.VMEM((TOK, HEADS * HDIM), BF16),
            pltpu.VMEM((ROWS, STEPS, HEADS * HDIM), BF16),
        ),
        in_specs=[any_spec] * 8 + [smem, smem],
        out_specs=(vspec, vspec),
        scratch_shapes=[
            vmem((NINST, 2, TOK, HDIM), BF16),
            vmem((TOK, HEADS * HDIM), BF16),
            vmem((ROWS, STEPS, HEADS * HDIM), BF16),
            vmem((ROWS, STEPS, HDIM), BF16),
            vmem((ROWS, STEPS, HDIM), BF16),
            vmem((ROWS, CACHE, HDIM), BF16),
            vmem((ROWS, CACHE, HDIM), BF16),
            vmem((HEADS, TOK, HDIM), BF16),
            vmem((HEADS, TOK, 2 * HDIM), F32),
            vmem((HEADS, TOK, HDIM), F32),
            vmem((2 * CHIP, 2 * HDIM), BF16),
            vmem((TOK, 2 * CHIP), F32),
            vmem((TOK, 2 * CHIP), F32),
            vmem((ROWS, per, HDIM), F32),
            vmem((ROWS, per, HDIM), BF16),
            vmem((ROWS, per, 2 * HDIM), F32),
            vmem((ROWS, per, HDIM), F32),
            vmem((ROWS * STEPS, HDIM), F32),
            vmem((ROWS * STEPS, HDIM), F32),
            pltpu.SemaphoreType.DMA((len(SENDS),)),
            pltpu.SemaphoreType.DMA((NINST, 2)),
            pltpu.SemaphoreType.DMA((len(CHIPS),)),
            pltpu.SemaphoreType.DMA((NINST,)),
            pltpu.SemaphoreType.DMA((8,)),
            pltpu.SemaphoreType.DMA((4, 2)),
        ],
        compiler_params=pltpu.CompilerParams(
            collective_id=0, has_side_effects=True, vmem_limit_bytes=56 * 2**20
        ),
    )(*args)


def solution(mesh):
    return jax.shard_map(
        per_device,
        mesh=mesh,
        in_specs=(
            P("inst", "tp"),
            P("inst", "tp"),
            P("inst", "tp"),
            P("inst", None, "tp"),
            P("inst", None, "tp"),
            P("inst", None, "tp"),
            P("inst", None, "tp"),
            P("inst", None, "tp"),
            P("inst"),
            P(),
        ),
        out_specs=(P("inst", "tp"), P("inst", None, "tp")),
        check_vma=False,
    )
```
